128 devices in a mesh: row: 32 (over x, z, core), col: 4 (over y).
Axes of the slice: x: 4, y: 4, z: 4, core: 2. Of those that a mesh axis runs over, the one named last changes fastest.
Arguments:
- front: float32 [8, 32, 128, 6144], P(None, 'row', None, 'col'), as said below
- child_tiles: bfloat16 [1024, 128, 6144], P('row', None, 'col'), may hold values from -0.75 to 0.75
- tile_parent: int32 [1024], P('row'), may hold values from 0 to 255, as said below
- tile_rows: int32 [1024, 128], P('row'), may hold values from -1 to 127, as said below
- tile_count: int32 [32], P('row'), may hold values from 24 to 32, as said below
Outputs:
- factored: float32 [8, 32, 128, 6144], P(None, 'row', None, 'col')
The draws below stay inside these ranges and needn't reach their ends.
Inputs may be any that keep to these rules, and one draw needn't show every extreme that they name: `tile_count`: the live slots of each index of row are the first ones, and one index has all 32 live. The live tiles of every index add into at most 2 parent row tiles t with the same t % 32; some value of t % 32 receives exactly 2 live tiles from every index of row. `tile_parent`: parent row tiles of the front. `tile_rows`: in each tile the non-negative positions are distinct. `front`: the first 1024 x 1024 block plus assembly stays positive definite.
All inputs are finite; a program needn't handle non-finite values.
Results may differ from the reference program's by a relative error of at most 0.00059.
Values may be sent and summed in bfloat16 or wider, within the bound.
No kernel may reach another device: no remote copies, remote signals or barrier semaphores. Data moves between devices by JAX's collectives and lax.ppermute only.
A program may use at most 256 MiB of HBM per device.

```python
import math
import jax
import jax.numpy as jnp
from jax import lax

F = 32768
P_SIZE = 1024
TILE_DEV = 32
CAP = 2
KB = 8
NT = 1024
C = 6144
N_ROW = 32


def lax_iota(length, axis):
    shape = [1, 1, 1, 1]
    shape[axis] = length
    return jnp.arange(length, dtype=jnp.int32).reshape(shape)


def draw_front(key, part):
    key = jax.random.fold_in(key, 14)
    first, second = jax.random.split(key)
    base = jax.random.uniform(first, (KB, N_ROW, 128, C), jnp.float32, -1.0, 1.0)
    boost = jax.random.uniform(second, (KB, N_ROW, 128, C), jnp.float32, 3.0, 6.0) * P_SIZE ** 0.5
    tile_k = lax_iota(KB, 0)
    tile_r = lax_iota(N_ROW, 1)
    inside = lax_iota(128, 2)
    column = lax_iota(C, 3)
    global_row = (tile_k * N_ROW + tile_r) * 128 + inside
    leading = (global_row < P_SIZE) & (column < P_SIZE)
    distance = jnp.abs(global_row - column).astype(jnp.float32)
    coupled = 3.0 * P_SIZE ** 0.5 * jnp.exp(distance * math.log(0.9))
    field = base + jnp.where(leading, coupled, 0.0)
    return jnp.where(global_row == column, field + boost, field)


def draw_tile_parent(key, part):
    key = jax.random.fold_in(key, 11)
    first, second, third = jax.random.split(key, 3)
    star = jax.random.randint(first, (), 0, N_ROW)
    scores = jax.random.randint(second, (N_ROW, N_ROW - 1), 0, 2 ** 20) * N_ROW + jnp.arange(N_ROW - 1, dtype=jnp.int32)[None, :]
    order = jnp.argsort(scores, axis=1, stable=True).astype(jnp.int32)
    others = (star + 1 + order) % N_ROW
    slots = jnp.arange(TILE_DEV, dtype=jnp.int32)
    group = jnp.clip((slots - CAP) // CAP, 0, N_ROW - 2)
    owner = jnp.where(slots[None, :] < CAP, star, others[:, group])
    local = jax.random.randint(third, (N_ROW, TILE_DEV), 0, KB)
    return (owner + N_ROW * local).reshape(-1).astype(jnp.int32)


def draw_tile_rows(key, part):
    key = jax.random.fold_in(key, 13)
    first, second = jax.random.split(key)
    scores = jax.random.randint(first, (NT, 128), 0, 2 ** 20) * 128 + jnp.arange(128, dtype=jnp.int32)[None, :]
    order = jnp.argsort(scores, axis=1, stable=True).astype(jnp.int32)
    lengths = jax.random.randint(second, (NT,), 32, 128)
    return jnp.where(jnp.arange(128, dtype=jnp.int32)[None, :] < lengths[:, None], order, -1).astype(jnp.int32)


def draw_tile_count(key, part):
    key = jax.random.fold_in(key, 12)
    first, second = jax.random.split(key)
    lowest = max(CAP, 3 * TILE_DEV // 4)
    counts = jax.random.randint(first, (N_ROW,), lowest, TILE_DEV + 1)
    busiest = jax.random.randint(second, (), 0, N_ROW)
    return jnp.where(jnp.arange(N_ROW, dtype=jnp.int32) == busiest, TILE_DEV, counts).astype(jnp.int32)


def levels(stream_key, dims, cuts, smallest, top_value):
    loudness, own = 1.0, jax.random.fold_in(stream_key, 6)
    for dim, parts in cuts:
        draws = jnp.exp(jax.random.uniform(jax.random.fold_in(own, dim), (parts,), jnp.float32, smallest / len(cuts), top_value / len(cuts)))
        loudness = loudness * jnp.repeat(draws, dims[dim] // parts).reshape([-1 if axis == dim else 1 for axis in range(len(dims))])
    return loudness


def centred(key, shape, spread, bound, cuts=(), kind=jnp.bfloat16):
    level = levels(key, shape, cuts, -0.22, 0.18) if cuts else 1.0
    array = jax.random.normal(key, shape, jnp.float32) * spread * level
    return jnp.minimum(jnp.maximum(array, -bound), bound).astype(kind)


def setup_inputs(seed: int = 0) -> dict:
    streams_of = jax.random.split(jax.random.key(seed), 6)
    return {
        "front": draw_front(jax.random.fold_in(streams_of[5], 71), 0),
        "child_tiles": centred(streams_of[1], (NT, 128, C), 0.25, 0.75, ((0, 32), (2, 4))),
        "tile_parent": draw_tile_parent(jax.random.fold_in(streams_of[5], 71), 0),
        "tile_rows": draw_tile_rows(jax.random.fold_in(streams_of[5], 71), 0),
        "tile_count": draw_tile_count(jax.random.fold_in(streams_of[5], 71), 0),
    }


def reference(front, child_tiles, tile_parent, tile_rows, tile_count):
    whole = front.reshape(F, C)
    slot_ids = jnp.arange(NT, dtype=jnp.int32)
    live = slot_ids % TILE_DEV < tile_count[slot_ids // TILE_DEV]
    target = tile_parent[:, None] * 128 + tile_rows
    target = jnp.where(live[:, None] & (tile_rows >= 0), target, F).astype(jnp.int32)

    def add_source(field, source):
        start = (source * TILE_DEV).astype(jnp.int32)
        pieces = lax.dynamic_slice_in_dim(child_tiles, start, TILE_DEV, 0)
        places = lax.dynamic_slice_in_dim(target, start, TILE_DEV, 0)
        values = pieces.reshape(TILE_DEV * 128, C).astype(jnp.float32)
        return (field.at[places.reshape(-1)].add(values, mode='drop'), None)
    assembled, _ = lax.scan(add_source, whole, jnp.arange(N_ROW, dtype=jnp.int32))
    diag_factor = jnp.linalg.cholesky(assembled[:P_SIZE, :P_SIZE])
    solved = jax.scipy.linalg.solve_triangular(diag_factor, assembled[P_SIZE:, :P_SIZE].T, lower=True).T
    panel = jnp.concatenate([diag_factor, solved], axis=0)
    panel_low = panel.astype(jnp.bfloat16)
    update = jnp.dot(panel_low.astype(jnp.float32), panel_low[:C].T.astype(jnp.float32), preferred_element_type=jnp.float32)
    factored = assembled - update
    factored = factored.at[:, :P_SIZE].set(panel)
    return factored.reshape(KB, N_ROW, 128, C)
```

```python
import jax
import jax.numpy as jnp
from jax import lax
from jax.experimental import pallas as pl
from jax.experimental.pallas import tpu as pltpu
from jax.sharding import PartitionSpec as P

PANEL = 1024
HIGH = lax.Precision.HIGHEST
f32 = jnp.float32
bf16 = jnp.bfloat16
MIB = 2**20


def times_transposed(a, b, precision=HIGH):
    return lax.dot_general(
        a, b, (((1,), (1,)), ((), ())), precision=precision, preferred_element_type=f32
    )


def times(a, b):
    return lax.dot_general(
        a, b, (((1,), (0,)), ((), ())), precision=HIGH, preferred_element_type=f32
    )


def place_kernel(rows_ref, child_ref, out_ref):
    width = out_ref.shape[-1]
    position = lax.broadcasted_iota(jnp.int32, (128, 128), 0)
    for slot in range(4):
        hot = jnp.where(rows_ref[0, slot : slot + 1, :] == position, 1.0, 0.0).astype(bf16)
        placed = jnp.dot(hot, child_ref[slot], preferred_element_type=f32).astype(bf16)
        for jp in range(8):
            for jc in range(4):
                out_ref[jp, jc, slot] = placed[
                    jp * 16 : jp * 16 + 16, jc * width : jc * width + width
                ]


def place(rows, child_tiles, width, block):
    slots = child_tiles.shape[0]
    return pl.pallas_call(
        place_kernel,
        grid=(slots // 4,),
        in_specs=[
            pl.BlockSpec((1, 4, 128), lambda t: (t, 0, 0)),
            pl.BlockSpec((4, 128, 4 * width), lambda t: (t, 0, block)),
        ],
        out_specs=pl.BlockSpec((8, 4, 4, 16, width), lambda t: (0, 0, t, 0, 0)),
        out_shape=jax.ShapeDtypeStruct((8, 4, slots, 16, width), bf16),
        compiler_params=pltpu.CompilerParams(vmem_limit_bytes=32 * MIB),
        cost_estimate=pl.CostEstimate(
            flops=2 * slots * 128 * 128 * 4 * width,
            bytes_accessed=2 * slots * 128 * 4 * width * 2,
            transcendentals=0,
        ),
        name="place_rows",
    )(rows.reshape(slots // 4, 4, 128), child_tiles)


def collect_kernel(at_ref, got_ref, out_ref):
    step = pl.program_id(0)

    @pl.when(step == 0)
    def _():
        out_ref[...] = jnp.zeros_like(out_ref)

    sources, slots = got_ref.shape[:2]

    def add(source, carry):
        base = (step * sources + source) * slots
        for slot in range(slots):
            at = at_ref[base + slot]
            out_ref[at] = out_ref[at] + got_ref[source, slot].astype(f32)
        return carry

    lax.fori_loop(0, sources, add, 0)


def collect(at, got):
    sources, slots, _, width = got.shape
    return pl.pallas_call(
        collect_kernel,
        grid_spec=pltpu.PrefetchScalarGridSpec(
            num_scalar_prefetch=1,
            grid=(sources // 4,),
            in_specs=[pl.BlockSpec((4, slots, 16, width), lambda s, at: (s, 0, 0, 0))],
            out_specs=pl.BlockSpec((256, 16, width), lambda s, at: (0, 0, 0)),
        ),
        out_shape=jax.ShapeDtypeStruct((256, 16, width), f32),
        compiler_params=pltpu.CompilerParams(vmem_limit_bytes=32 * MIB),
        cost_estimate=pl.CostEstimate(
            flops=sources * slots * 16 * width,
            bytes_accessed=sources * slots * 16 * width * 2 + 256 * 16 * width * 4,
            transcendentals=0,
        ),
        name="collect_parents",
    )(at, got)


def factor_block(block, u_ref, w_ref):
    sub = lax.broadcasted_iota(jnp.int32, (8, 128), 0)
    lane = lax.broadcasted_iota(jnp.int32, (8, 128), 1)
    s = [block[8 * g : 8 * g + 8, :] for g in range(16)]
    v = [jnp.where(lane == sub + 8 * g, 1.0, 0.0).astype(f32) for g in range(16)]
    for k in range(128):
        g0, s0 = divmod(k, 8)
        cols = [jnp.broadcast_to(s[g][:, k : k + 1], (8, 128)) for g in range(g0, 16)]
        pivot = jnp.broadcast_to(cols[0][s0 : s0 + 1, :], (8, 128))
        inverse = 1.0 / pivot
        row = jnp.broadcast_to(s[g0][s0 : s0 + 1, :], (8, 128))
        vrow = jnp.broadcast_to(v[g0][s0 : s0 + 1, :], (8, 128))
        root = lax.rsqrt(pivot)
        root = root * (1.5 - 0.5 * pivot * root * root)
        u_ref[k : k + 1, :] = jnp.where(lane >= k, row * root, 0.0)[:1]
        w_ref[k : k + 1, :] = (vrow * root)[:1]
        row, vrow = row * inverse, vrow * inverse
        for g in range(g0, 16):
            if g == g0 and s0 == 7:
                continue
            col = cols[g - g0]
            if g == g0:
                col = jnp.where(sub > s0, col, 0.0)
            s[g] = s[g] - col * row
            v[g] = v[g] - col * vrow


def factor_kernel(pieces_ref, l_ref, x_ref, a_ref, u_ref, w_ref):
    for jp in range(8):
        for jc in range(4):
            for tile in range(8):
                at = tile * 128 + jp * 16
                a_ref[at : at + 16, jc * 256 : jc * 256 + 256] = pieces_ref[jp * 4 + jc, tile]
    l_ref[...] = jnp.zeros_like(l_ref)
    x_ref[...] = jnp.zeros_like(x_ref)
    for i in range(8):
        for j in range(i + 1):
            bi, bj = slice(128 * i, 128 * i + 128), slice(128 * j, 128 * j + 128)
            a_ref[bi, bj] = 0.5 * (a_ref[bi, bj] + a_ref[bj, bi].T)

    def step(b, carry):
        at = pl.ds(pl.multiple_of(b * 128, 128), 128)
        factor_block(a_ref[at, at], u_ref, w_ref)
        w = w_ref[...]
        l_ref[at, at] = u_ref[...].T
        x_ref[at, at] = w
        for n in range(8):

            @pl.when(b == n)
            def _():
                here = slice(128 * n, 128 * n + 128)
                if n < 7:
                    below = slice(128 * n + 128, PANEL)
                    low = times_transposed(a_ref[below, here], w)
                    l_ref[below, here] = low
                    for j in range(n + 1, 8):
                        rows, cols = slice(128 * j, PANEL), slice(128 * j, 128 * j + 128)
                        off = 128 * (j - n - 1)
                        a_ref[rows, cols] = a_ref[rows, cols] - times_transposed(
                            low[off:], low[off : off + 128]
                        )
                if n > 0:
                    done = slice(0, 128 * n)
                    x_ref[here, done] = -times(w, times(l_ref[here, done], x_ref[done, done]))

        return carry

    lax.fori_loop(0, 8, step, 0)


def factor(pieces):
    return pl.pallas_call(
        factor_kernel,
        out_shape=[jax.ShapeDtypeStruct((PANEL, PANEL), f32)] * 2,
        scratch_shapes=[
            pltpu.VMEM((PANEL, PANEL), f32),
            pltpu.VMEM((128, 128), f32),
            pltpu.VMEM((128, 128), f32),
        ],
        compiler_params=pltpu.CompilerParams(vmem_limit_bytes=40 * MIB),
        cost_estimate=pl.CostEstimate(
            flops=10**11, bytes_accessed=12 * MIB, transcendentals=0
        ),
        name="factor_and_invert",
    )(pieces)


def finish_kernel(col_ref, panel_ref, lower_ref, front_ref, got_ref, spread_ref, slab_ref, out_ref):
    tiles = panel_ref.shape[0]
    rows = spread_ref[...].reshape(tiles * 128, PANEL)

    @pl.when(col_ref[0] == 0)
    def _():
        out_ref[:, 0, :, :PANEL] = lower_ref[...]

    @pl.when(col_ref[0] != 0)
    def _():
        update = times_transposed(rows, slab_ref[:PANEL, :], None)
        out_ref[:, 0, :, :PANEL] = panel_ref[...] - update.reshape(tiles, 128, PANEL)

    update = times_transposed(rows, slab_ref[PANEL:, :], None).reshape(tiles, 128, -1)
    for jc in range(4):
        for tile in range(tiles):
            cols = slice(jc * 128, jc * 128 + 128)
            sums = got_ref[:, jc, tile].reshape(128, 128)
            out_ref[tile, 0, :, PANEL + jc * 128 : PANEL + jc * 128 + 128] = (
                front_ref[tile, 0, :, cols] + sums - update[tile, :, cols]
            )


def finish(col_index, panel, lower, front, got, spread, slab):
    k, _, _, width = front.shape
    step = 2
    return pl.pallas_call(
        finish_kernel,
        grid_spec=pltpu.PrefetchScalarGridSpec(
            num_scalar_prefetch=1,
            grid=(k // step,),
            in_specs=[
                pl.BlockSpec((step, 128, PANEL), lambda i, c: (i, 0, 0)),
                pl.BlockSpec((step, 128, PANEL), lambda i, c: (i, 0, 0)),
                pl.BlockSpec((step, 1, 128, 512), lambda i, c: (i, 0, 0, 2)),
                pl.BlockSpec((8, 4, step, 16, 128), lambda i, c: (0, 0, i, 0, 0)),
                pl.BlockSpec((step, 128, PANEL), lambda i, c: (i, 0, 0)),
                pl.BlockSpec((width, PANEL), lambda i, c: (0, 0)),
            ],
            out_specs=pl.BlockSpec((step, 1, 128, width), lambda i, c: (i, 0, 0, 0)),
        ),
        out_shape=jax.ShapeDtypeStruct(front.shape, f32),
        compiler_params=pltpu.CompilerParams(vmem_limit_bytes=40 * MIB),
        cost_estimate=pl.CostEstimate(
            flops=2 * k * 128 * width * PANEL,
            bytes_accessed=28 * MIB,
            transcendentals=0,
        ),
        name="trailing_update",
    )(col_index.reshape(1), panel, lower, front, got, spread, slab)


def exchange(x, groups=None, axis="row"):
    return lax.all_to_all(
        x, axis, split_axis=0, concat_axis=0, axis_index_groups=groups, tiled=True
    )


def gather_rows(x, row_index):
    chips = lax.axis_size("row") // 2
    groups = [[2 * chip + core for chip in range(chips)] for core in range(2)]
    mine = exchange(jnp.broadcast_to(x[None], (chips,) + x.shape), groups)
    other = lax.ppermute(mine, "row", [(r, r ^ 1) for r in range(2 * chips)])
    first = row_index % 2 == 0
    both = jnp.stack([jnp.where(first, mine, other), jnp.where(first, other, mine)], axis=1)
    return both.reshape((2 * chips,) + x.shape)


def from_first(pieces, col_index):
    result = jnp.where(col_index == 0, pieces[0], 0)
    for c in range(1, len(pieces)):
        result = result + lax.ppermute(pieces[c], "col", [(0, c)])
    return result


def body(front, child_tiles, tile_parent, tile_rows, tile_count):
    row_index = lax.axis_index("row")
    col_index = lax.axis_index("col")
    slots = child_tiles.shape[0]
    live = jnp.arange(slots, dtype=jnp.int32) < tile_count[0]
    rows = jnp.where(live[:, None], tile_rows, -1)
    at = (tile_parent % 32) * 8 + tile_parent // 32
    at = exchange(jnp.broadcast_to(at[None], (32, slots))).reshape(32 * slots)

    early = front[:2, 0, :, :PANEL].reshape(2, 8, 16, 4, 256).transpose(1, 3, 0, 2, 4)
    early = exchange(early.reshape(32, 2, 16, 256))

    sent_panel = place(rows, child_tiles, 256, 0).reshape(32, slots, 16, 256)
    sums_panel = collect(at, exchange(sent_panel))
    sent_rest = place(rows, child_tiles, 128, 2).reshape(32, slots, 16, 128)
    sums_rest = collect(at, exchange(sent_rest))

    sums = sums_panel.reshape(32, 8, 16, 256)
    tiles = (sums[:, :2] + early).transpose(1, 0, 2, 3).reshape(64, 16, 256)
    pieces = [jnp.concatenate([tiles[:8], tiles[12 * c : 12 * c + 12]]) for c in range(4)]
    piece = from_first(pieces, col_index)
    diagonal = gather_rows(piece[:8], row_index)
    quads = [[4 * q + i for i in range(4)] for q in range(8)]
    part = exchange(piece[8:].reshape(4, 3, 16, 256), quads)
    part = part.transpose(1, 2, 0, 3).reshape(48, PANEL)

    got = exchange(sums).reshape(8, 4, 8, 16, 256).transpose(2, 0, 3, 1, 4)
    panel = front[:, 0, :, :PANEL] + got.reshape(8, 128, PANEL)
    own = from_first([panel[2 * c : 2 * c + 2] for c in range(4)], col_index)

    factored, inverse = factor(diagonal)

    def rows_of_factor(start, count):
        start = jnp.minimum(start, PANEL - count)
        return lax.dynamic_slice_in_dim(factored, start, count, 0)

    in_factor = row_index < 8
    top = rows_of_factor(row_index * 128, 128)
    own = times_transposed(own.reshape(256, PANEL), inverse)
    own = own.at[:128].set(jnp.where(in_factor & (col_index == 0), top, own[:128]))
    own = own.astype(bf16)
    spread = exchange(jnp.broadcast_to(own[None], (4, 256, PANEL)), None, "col")
    spread = spread.reshape(8, 128, PANEL)

    part = times_transposed(part, inverse).reshape(3, 16, PANEL)
    for q in range(3):
        tile = 12 * col_index + 3 * (row_index % 4) + q
        known = rows_of_factor(tile * 128 + row_index // 4 * 16, 16)
        part = part.at[q].set(jnp.where(tile < 8, known, part[q]))
    slab = gather_rows(part.astype(bf16), row_index)
    slab = slab.reshape(8, 4, 3, 16, PANEL).transpose(1, 2, 0, 3, 4).reshape(1536, PANEL)

    lower = times_transposed(panel.reshape(8 * 128, PANEL), inverse).reshape(8, 128, PANEL)
    lower = lower.at[0].set(jnp.where(in_factor, top, lower[0]))

    got_rest = exchange(sums_rest.reshape(32, 8, 16, 128)).reshape(8, 4, 8, 16, 128)
    return finish(col_index, panel, lower, front, got_rest, spread, slab)


def solution(mesh):
    placed = (
        P(None, "row", None, "col"),
        P("row", None, "col"),
        P("row"),
        P("row", None),
        P("row"),
    )
    return jax.shard_map(
        body, mesh=mesh, in_specs=placed, out_specs=P(None, "row", None, "col"), check_vma=False
    )
```

```python
import jax
import jax.numpy as jnp
from jax import lax
from jax.experimental import pallas as pl
from jax.experimental.pallas import tpu as pltpu
from jax.sharding import PartitionSpec as P

PANEL = 1024
HIGH = lax.Precision.HIGHEST
f32 = jnp.float32
bf16 = jnp.bfloat16
MIB = 2**20


def times_transposed(a, b, precision=HIGH):
    return lax.dot_general(
        a, b, (((1,), (1,)), ((), ())), precision=precision, preferred_element_type=f32
    )


def times(a, b):
    return lax.dot_general(
        a, b, (((1,), (0,)), ((), ())), precision=HIGH, preferred_element_type=f32
    )


def place_kernel(rows_ref, child_ref, out_ref):
    width = out_ref.shape[-1]
    position = lax.broadcasted_iota(jnp.int32, (128, 128), 0)
    for slot in range(4):
        hot = jnp.where(rows_ref[0, slot : slot + 1, :] == position, 1.0, 0.0).astype(bf16)
        placed = jnp.dot(hot, child_ref[slot], preferred_element_type=f32).astype(bf16)
        for jp in range(8):
            for jc in range(4):
                out_ref[jp, jc, slot] = placed[
                    jp * 16 : jp * 16 + 16, jc * width : jc * width + width
                ]


def place(rows, child_tiles, width, block):
    slots = child_tiles.shape[0]
    return pl.pallas_call(
        place_kernel,
        grid=(slots // 4,),
        in_specs=[
            pl.BlockSpec((1, 4, 128), lambda t: (t, 0, 0)),
            pl.BlockSpec((4, 128, 4 * width), lambda t: (t, 0, block)),
        ],
        out_specs=pl.BlockSpec((8, 4, 4, 16, width), lambda t: (0, 0, t, 0, 0)),
        out_shape=jax.ShapeDtypeStruct((8, 4, slots, 16, width), bf16),
        compiler_params=pltpu.CompilerParams(vmem_limit_bytes=56 * MIB),
        cost_estimate=pl.CostEstimate(
            flops=2 * slots * 128 * 128 * 4 * width,
            bytes_accessed=2 * slots * 128 * 4 * width * 2,
            transcendentals=0,
        ),
        name="place_rows",
    )(rows.reshape(slots // 4, 4, 128), child_tiles)


def collect_kernel(at_ref, got_ref, out_ref):
    step = pl.program_id(0)

    @pl.when(step == 0)
    def _():
        out_ref[...] = jnp.zeros_like(out_ref)

    sources, slots = got_ref.shape[:2]

    def add(source, carry):
        base = (step * sources + source) * slots
        for slot in range(slots):
            at = at_ref[base + slot]
            out_ref[at] = out_ref[at] + got_ref[source, slot].astype(f32)
        return carry

    lax.fori_loop(0, sources, add, 0)


def collect(at, got):
    sources, slots, _, width = got.shape
    return pl.pallas_call(
        collect_kernel,
        grid_spec=pltpu.PrefetchScalarGridSpec(
            num_scalar_prefetch=1,
            grid=(sources // 4,),
            in_specs=[pl.BlockSpec((4, slots, 16, width), lambda s, at: (s, 0, 0, 0))],
            out_specs=pl.BlockSpec((256, 16, width), lambda s, at: (0, 0, 0)),
        ),
        out_shape=jax.ShapeDtypeStruct((256, 16, width), f32),
        compiler_params=pltpu.CompilerParams(vmem_limit_bytes=56 * MIB),
        cost_estimate=pl.CostEstimate(
            flops=sources * slots * 16 * width,
            bytes_accessed=sources * slots * 16 * width * 2 + 256 * 16 * width * 4,
            transcendentals=0,
        ),
        name="collect_parents",
    )(at, got)


def factor_block(block, u_ref, w_ref):
    sub = lax.broadcasted_iota(jnp.int32, (8, 128), 0)
    lane = lax.broadcasted_iota(jnp.int32, (8, 128), 1)

    def full(x):
        return jnp.broadcast_to(x, (8, 128))

    s = [block[8 * g : 8 * g + 8, :] for g in range(16)]
    v = [jnp.where(lane == sub + 8 * g, 1.0, 0.0).astype(f32) for g in range(16)]
    for b in range(16):
        cols = [full(s[b][:, 8 * b + j : 8 * b + j + 1]) for j in range(8)]
        e = [[full(cols[j][i : i + 1, :]) for j in range(i + 1)] for i in range(8)]
        inv, w, roots = [], [], []
        f = [[None] * 8 for _ in range(8)]
        for t in range(8):
            pivot = e[t][t]
            inv.append(1.0 / pivot)
            root = lax.rsqrt(pivot)
            roots.append(root * (1.5 - 0.5 * pivot * root * root))
            for i in range(t + 1, 8):
                f[i][t] = e[i][t] * inv[t]
            for i in range(t + 1, 8):
                for j in range(t + 1, i + 1):
                    e[i][j] = e[i][j] - f[i][t] * e[j][t]
        for i in range(8):
            r = []
            for j in range(i):
                acc = f[i][j]
                for k in range(j + 1, i):
                    acc = acc + f[i][k] * w[k][j]
                r.append(-acc)
            w.append(r)
        rows, vrows = s[b], v[b]
        new, vnew, scale = rows, vrows, roots[0]
        for i in range(1, 8):
            scale = jnp.where(sub == i, roots[i], scale)
        for j in range(7):
            c = jnp.zeros((8, 128), f32)
            for i in range(j + 1, 8):
                c = jnp.where(sub == i, w[i][j], c)
            new = new + c * full(rows[j : j + 1, :])
            vnew = vnew + c * full(vrows[j : j + 1, :])
        u_ref[8 * b : 8 * b + 8, :] = jnp.where(lane >= sub + 8 * b, new * scale, 0.0)
        w_ref[8 * b : 8 * b + 8, :] = vnew * scale
        if b == 15:
            break
        wi = [[w[t][j] * inv[t] for j in range(t)] for t in range(8)]
        brow = [full(new[t : t + 1, :]) for t in range(8)]
        bvrow = [full(vnew[t : t + 1, :]) for t in range(8)]
        for g in range(b + 1, 16):
            c = [full(s[g][:, 8 * b + j : 8 * b + j + 1]) for j in range(8)]
            for t in range(8):
                m = inv[t] * c[t]
                for j in range(t):
                    m = m + wi[t][j] * c[j]
                s[g] = s[g] - m * brow[t]
                v[g] = v[g] - m * bvrow[t]


def factor_kernel(index_ref, mine_ref, other_ref, l_ref, x_ref, a_ref, u_ref, w_ref):
    for half, ref in enumerate((mine_ref, other_ref)):
        for n in range(16):
            j = index_ref[half * 16 + n]
            cols = pl.ds(pl.multiple_of(j % 4 * 256, 256), 256)
            for tile in range(8):
                rows = pl.ds(pl.multiple_of(tile * 128 + j // 4 * 16, 16), 16)
                a_ref[rows, cols] = ref[n // 4, n % 4, tile]
    l_ref[...] = jnp.zeros_like(l_ref)
    x_ref[...] = jnp.zeros_like(x_ref)
    for i in range(8):
        for j in range(i + 1):
            bi, bj = slice(128 * i, 128 * i + 128), slice(128 * j, 128 * j + 128)
            a_ref[bi, bj] = 0.5 * (a_ref[bi, bj] + a_ref[bj, bi].T)

    def step(b, carry):
        at = pl.ds(pl.multiple_of(b * 128, 128), 128)
        factor_block(a_ref[at, at], u_ref, w_ref)
        w = w_ref[...]
        l_ref[at, at] = u_ref[...].T
        x_ref[at, at] = w
        for n in range(8):

            @pl.when(b == n)
            def _():
                here = slice(128 * n, 128 * n + 128)
                if n < 7:
                    below = slice(128 * n + 128, PANEL)
                    low = times_transposed(a_ref[below, here], w)
                    l_ref[below, here] = low
                    for j in range(n + 1, 8):
                        rows, cols = slice(128 * j, PANEL), slice(128 * j, 128 * j + 128)
                        off = 128 * (j - n - 1)
                        a_ref[rows, cols] = a_ref[rows, cols] - times_transposed(
                            low[off:], low[off : off + 128]
                        )
                if n > 0:
                    done = slice(0, 128 * n)
                    x_ref[here, done] = -times(w, times(l_ref[here, done], x_ref[done, done]))

        return carry

    lax.fori_loop(0, 8, step, 0)


def factor(index, mine, other):
    whole = pl.BlockSpec(memory_space=pltpu.VMEM)
    return pl.pallas_call(
        factor_kernel,
        in_specs=[pl.BlockSpec(memory_space=pltpu.SMEM), whole, whole],
        out_specs=[whole, whole],
        out_shape=[jax.ShapeDtypeStruct((PANEL, PANEL), f32)] * 2,
        scratch_shapes=[
            pltpu.VMEM((PANEL, PANEL), f32),
            pltpu.VMEM((128, 128), f32),
            pltpu.VMEM((128, 128), f32),
        ],
        compiler_params=pltpu.CompilerParams(vmem_limit_bytes=40 * MIB),
        cost_estimate=pl.CostEstimate(
            flops=7 * 10**10, bytes_accessed=12 * MIB, transcendentals=0
        ),
        name="factor_and_invert",
    )(index, mine, other)


def assemble_kernel(front_ref, got_ref, out_ref):
    for jc in range(4):
        cols = slice(jc * 256, jc * 256 + 256)
        out_ref[0, :, cols] = front_ref[0, 0, :, cols] + got_ref[:, jc, 0].reshape(128, 256)


def assemble(front, got):
    k = front.shape[0]
    return pl.pallas_call(
        assemble_kernel,
        grid=(k,),
        in_specs=[
            pl.BlockSpec((1, 1, 128, PANEL), lambda i: (i, 0, 0, 0)),
            pl.BlockSpec((8, 4, 1, 16, 256), lambda i: (0, 0, i, 0, 0)),
        ],
        out_specs=pl.BlockSpec((1, 128, PANEL), lambda i: (i, 0, 0)),
        out_shape=jax.ShapeDtypeStruct((k, 128, PANEL), f32),
        compiler_params=pltpu.CompilerParams(vmem_limit_bytes=56 * MIB),
        cost_estimate=pl.CostEstimate(
            flops=k * 128 * PANEL, bytes_accessed=12 * MIB, transcendentals=0
        ),
        name="assemble_panel",
    )(front, got)


def finish_kernel(
    order_ref, index_ref, panel_ref, lower_ref, top_ref, front_ref, got_ref, spread_ref,
    mine_ref, other_ref, out_ref, slab_ref,
):
    step = pl.program_id(0)
    tiles = panel_ref.shape[0]
    leading = order_ref[4] == 0

    @pl.when(step == 0)
    def _():
        for half, ref in enumerate((mine_ref, other_ref)):
            for n in range(16):
                j = index_ref[half * 16 + n]
                for q in range(3):
                    at = (j % 4 * 3 + q) * 128 + j // 4 * 16
                    slab_ref[pl.ds(pl.multiple_of(at, 16), 16), :] = ref[n // 4, n % 4, q]

    rows = spread_ref[0]

    @pl.when(leading)
    def _():
        out_ref[:, 0, :, :PANEL] = lower_ref[...]

    @pl.when(leading & (order_ref[step] == 0) & (order_ref[5] < 8))
    def _():
        out_ref[0, 0, :, :PANEL] = top_ref[...]

    @pl.when(jnp.logical_not(leading))
    def _():
        update = times_transposed(rows, slab_ref[:PANEL, :], None)
        out_ref[:, 0, :, :PANEL] = panel_ref[...] - update.reshape(tiles, 128, PANEL)

    update = times_transposed(rows, slab_ref[PANEL:, :], None).reshape(tiles, 128, -1)
    for jc in range(4):
        for tile in range(tiles):
            cols = slice(jc * 128, jc * 128 + 128)
            sums = got_ref[:, jc, tile].reshape(128, 128)
            out_ref[tile, 0, :, PANEL + jc * 128 : PANEL + jc * 128 + 128] = (
                front_ref[tile, 0, :, cols] + sums - update[tile, :, cols]
            )


def finish(order, index, panel, lower, top, front, got, spread, mine, other):
    k, _, _, width = front.shape
    step = k // 4
    return pl.pallas_call(
        finish_kernel,
        grid_spec=pltpu.PrefetchScalarGridSpec(
            num_scalar_prefetch=2,
            grid=(4,),
            in_specs=[
                pl.BlockSpec((step, 128, PANEL), lambda i, o, _: (o[i], 0, 0)),
                pl.BlockSpec((step, 128, PANEL), lambda i, o, _: (o[i], 0, 0)),
                pl.BlockSpec((128, PANEL), lambda i, o, _: (0, 0)),
                pl.BlockSpec((step, 1, 128, 512), lambda i, o, _: (o[i], 0, 0, 2)),
                pl.BlockSpec((8, 4, step, 16, 128), lambda i, o, _: (0, 0, o[i], 0, 0)),
                pl.BlockSpec((1, step * 128, PANEL), lambda i, o, _: (i, 0, 0)),
                pl.BlockSpec(mine.shape, lambda i, o, _: (0, 0, 0, 0, 0)),
                pl.BlockSpec(other.shape, lambda i, o, _: (0, 0, 0, 0, 0)),
            ],
            out_specs=pl.BlockSpec((step, 1, 128, width), lambda i, o, _: (o[i], 0, 0, 0)),
            scratch_shapes=[pltpu.VMEM((width, PANEL), bf16)],
        ),
        out_shape=jax.ShapeDtypeStruct(front.shape, f32),
        compiler_params=pltpu.CompilerParams(vmem_limit_bytes=48 * MIB),
        cost_estimate=pl.CostEstimate(
            flops=2 * k * 128 * width * PANEL,
            bytes_accessed=28 * MIB,
            transcendentals=0,
        ),
        name="trailing_update",
    )(order, index, panel, lower, top, front, got, spread, mine, other)


def exchange(x):
    return lax.all_to_all(x, "row", split_axis=0, concat_axis=0, tiled=True)


def row_number(x, z, core):
    return (x % 4 * 4 + z % 4) * 2 + core


def ring_stage(x, stage):
    parts = [x]
    for by in range(1, 4):
        moves = []
        for chip in range(16):
            for core in range(2):
                along_z = core == stage
                to = row_number(
                    chip // 4 + (0 if along_z else by), chip % 4 + (by if along_z else 0), core
                )
                moves.append((chip * 2 + core, to))
        parts.append(lax.ppermute(x, "row", moves))
    return jnp.stack(parts)


def gather_rows(x):
    mine = ring_stage(ring_stage(x, 0), 1)
    other = lax.ppermute(mine, "row", [(r, r ^ 1) for r in range(32)])
    return mine, other


def gathered_index(row_index):
    number = jnp.arange(32, dtype=jnp.int32)
    half, outer, inner = number // 16, number // 4 % 4, number % 4
    core = (row_index + half) % 2
    chip = row_index // 2
    x = chip // 4 - jnp.where(core == 0, outer, inner) + 4
    z = chip % 4 - jnp.where(core == 0, inner, outer) + 4
    return row_number(x, z, core)


def from_first(pieces, col_index):
    result = jnp.where(col_index == 0, pieces[0], 0)
    for c in range(1, len(pieces)):
        result = result + lax.ppermute(pieces[c], "col", [(0, c)])
    return result


def own_rows(tiles, row_index):
    tiles = tiles.reshape(4, 3, 16, 256)
    quarter = row_index % 4
    result = jnp.zeros((3, 16, PANEL), f32)
    for by in range(4):
        part = lax.dynamic_index_in_dim(tiles, quarter ^ by, 0, keepdims=False)
        if by:
            part = lax.ppermute(part, "row", [(r, r ^ by) for r in range(32)])
        result = lax.dynamic_update_slice(result, part, (0, 0, (quarter ^ by) * 256))
    return result.reshape(48, PANEL)


def together(*arrays):
    return lax.optimization_barrier(arrays)


def body(front, child_tiles, tile_parent, tile_rows, tile_count):
    row_index = lax.axis_index("row").astype(jnp.int32)
    col_index = lax.axis_index("col").astype(jnp.int32)
    slots = child_tiles.shape[0]
    index = gathered_index(row_index)
    live = jnp.arange(slots, dtype=jnp.int32) < tile_count[0]
    rows = jnp.where(live[:, None], tile_rows, -1)
    at = (tile_parent % 32) * 8 + tile_parent // 32
    at = lax.all_gather(at, "row", axis=0, tiled=True)

    early = front[:2, 0, :, :PANEL].reshape(2, 8, 16, 4, 256).transpose(1, 3, 0, 2, 4)
    early = exchange(early.reshape(32, 2, 16, 256))

    sent = place(rows, child_tiles, 256, 0).reshape(32, slots, 16, 256)
    sent, early = together(sent, early)
    sums = collect(at, exchange(sent)).reshape(32, 8, 16, 256)
    sent_rest = place(rows, child_tiles, 128, 2).reshape(32, slots, 16, 128)

    tiles = (sums[:, :2] + early).transpose(1, 0, 2, 3).reshape(64, 16, 256)
    diagonal = from_first([tiles[:8]] * 4, col_index)
    part = from_first([tiles[12 * c : 12 * c + 12] for c in range(4)], col_index)
    diagonal = gather_rows(diagonal)
    part = own_rows(part, row_index)

    got, sent_rest = together(exchange(sums), sent_rest)
    panel = assemble(front, got.reshape(8, 4, 8, 16, 256))
    own = from_first([panel[2 * c : 2 * c + 2] for c in range(4)], col_index)
    got_rest = exchange(sent_rest)

    factored, inverse = factor(index, *diagonal)

    def rows_of_factor(start, count):
        start = jnp.minimum(start, PANEL - count)
        return lax.dynamic_slice_in_dim(factored, start, count, 0)

    part = times_transposed(part, inverse).reshape(3, 16, PANEL)
    known, tile = [], 12 * col_index + 3 * (row_index % 4)
    for q in range(3):
        known.append(rows_of_factor((tile + q) * 128 + row_index // 4 * 16, 16))
    inside = tile + jnp.arange(3, dtype=jnp.int32) < 8
    part = jnp.where(inside[:, None, None], jnp.stack(known), part).astype(bf16)
    slab = gather_rows(part)

    top = rows_of_factor(row_index * 128, 128)
    own = times_transposed(own.reshape(256, PANEL), inverse)
    inside = (jnp.arange(256) < 128) & (row_index < 8) & (col_index == 0)
    own = jnp.where(inside[:, None], jnp.concatenate([top, top]), own).astype(bf16)
    spread = jnp.stack(
        [own] + [lax.ppermute(own, "col", [(c, (c + s) % 4) for c in range(4)]) for s in (1, 2, 3)]
    )

    got_rest, inverse, _, _ = together(got_rest, inverse, part, own)
    sums_rest = collect(at, got_rest)
    got_rest = exchange(sums_rest.reshape(32, 8, 16, 128)).reshape(8, 4, 8, 16, 128)
    lower = times_transposed(panel.reshape(8 * 128, PANEL), inverse).reshape(8, 128, PANEL)

    order = (col_index + 4 - jnp.arange(4, dtype=jnp.int32)) % 4
    order = jnp.concatenate([order, jnp.stack([col_index, row_index])])
    return finish(order, index, panel, lower, top, front, got_rest, spread, *slab)


def solution(mesh):
    placed = (
        P(None, "row", None, "col"),
        P("row", None, "col"),
        P("row"),
        P("row", None),
        P("row"),
    )
    return jax.shard_map(
        body, mesh=mesh, in_specs=placed, out_specs=P(None, "row", None, "col"), check_vma=False
    )
```

```python
import jax
import jax.numpy as jnp
from jax import lax
from jax.experimental import pallas as pl
from jax.experimental.pallas import tpu as pltpu
from jax.sharding import PartitionSpec as P

PANEL = 1024
HIGH = lax.Precision.HIGHEST
f32 = jnp.float32
bf16 = jnp.bfloat16
MIB = 2**20


def times_transposed(a, b, precision=HIGH):
    return lax.dot_general(
        a, b, (((1,), (1,)), ((), ())), precision=precision, preferred_element_type=f32
    )


def times(a, b):
    return lax.dot_general(
        a, b, (((1,), (0,)), ((), ())), precision=HIGH, preferred_element_type=f32
    )


def place_kernel(rows_ref, child_ref, out_ref):
    width = out_ref.shape[-1]
    position = lax.broadcasted_iota(jnp.int32, (128, 128), 0)
    for slot in range(4):
        hot = jnp.where(rows_ref[0, slot : slot + 1, :] == position, 1.0, 0.0).astype(bf16)
        placed = jnp.dot(hot, child_ref[slot], preferred_element_type=f32).astype(bf16)
        for jp in range(8):
            for jc in range(4):
                out_ref[jp, jc, slot] = placed[
                    jp * 16 : jp * 16 + 16, jc * width : jc * width + width
                ]


def place(rows, child_tiles, width, block):
    slots = child_tiles.shape[0]
    return pl.pallas_call(
        place_kernel,
        grid=(slots // 4,),
        in_specs=[
            pl.BlockSpec((1, 4, 128), lambda t: (t, 0, 0)),
            pl.BlockSpec((4, 128, 4 * width), lambda t: (t, 0, block)),
        ],
        out_specs=pl.BlockSpec((8, 4, 4, 16, width), lambda t: (0, 0, t, 0, 0)),
        out_shape=jax.ShapeDtypeStruct((8, 4, slots, 16, width), bf16),
        compiler_params=pltpu.CompilerParams(vmem_limit_bytes=56 * MIB),
        cost_estimate=pl.CostEstimate(
            flops=2 * slots * 128 * 128 * 4 * width,
            bytes_accessed=2 * slots * 128 * 4 * width * 2,
            transcendentals=0,
        ),
        name="place_rows",
    )(rows.reshape(slots // 4, 4, 128), child_tiles)


def collect_kernel(at_ref, got_ref, *refs):
    out_ref = refs[-1]
    step = pl.program_id(0)

    @pl.when(step == 0)
    def _():
        out_ref[...] = jnp.zeros_like(out_ref)

    sources, slots = got_ref.shape[:2]

    def add(source, carry):
        base = (step * sources + source) * slots
        for slot in range(slots):
            at = at_ref[base + slot]
            out_ref[at] = out_ref[at] + got_ref[source, slot].astype(f32)
        return carry

    lax.fori_loop(0, sources, add, 0)


def collect(at, got, *after):
    sources, slots, _, width = got.shape
    return pl.pallas_call(
        collect_kernel,
        grid_spec=pltpu.PrefetchScalarGridSpec(
            num_scalar_prefetch=1,
            grid=(sources // 4,),
            in_specs=[pl.BlockSpec((4, slots, 16, width), lambda s, at: (s, 0, 0, 0))]
            + [pl.BlockSpec(memory_space=pl.ANY)] * len(after),
            out_specs=pl.BlockSpec((256, 16, width), lambda s, at: (0, 0, 0)),
        ),
        out_shape=jax.ShapeDtypeStruct((256, 16, width), f32),
        compiler_params=pltpu.CompilerParams(vmem_limit_bytes=56 * MIB),
        cost_estimate=pl.CostEstimate(
            flops=sources * slots * 16 * width,
            bytes_accessed=sources * slots * 16 * width * 2 + 256 * 16 * width * 4,
            transcendentals=0,
        ),
        name="collect_parents",
    )(at, got, *after)


def factor_block(block, u_ref, w_ref):
    sub = lax.broadcasted_iota(jnp.int32, (8, 128), 0)
    lane = lax.broadcasted_iota(jnp.int32, (8, 128), 1)

    def full(x):
        return jnp.broadcast_to(x, (8, 128))

    s = [block[8 * g : 8 * g + 8, :] for g in range(16)]
    v = [jnp.where(lane == sub + 8 * g, 1.0, 0.0).astype(f32) for g in range(16)]
    for b in range(16):
        cols = [full(s[b][:, 8 * b + j : 8 * b + j + 1]) for j in range(8)]
        e = [[full(cols[j][i : i + 1, :]) for j in range(i + 1)] for i in range(8)]
        inv, w, roots = [], [], []
        f = [[None] * 8 for _ in range(8)]
        for t in range(8):
            pivot = e[t][t]
            inv.append(1.0 / pivot)
            root = lax.rsqrt(pivot)
            roots.append(root * (1.5 - 0.5 * pivot * root * root))
            for i in range(t + 1, 8):
                f[i][t] = e[i][t] * inv[t]
            for i in range(t + 1, 8):
                for j in range(t + 1, i + 1):
                    e[i][j] = e[i][j] - f[i][t] * e[j][t]
        for i in range(8):
            r = []
            for j in range(i):
                acc = f[i][j]
                for k in range(j + 1, i):
                    acc = acc + f[i][k] * w[k][j]
                r.append(-acc)
            w.append(r)
        rows, vrows = s[b], v[b]
        new, vnew, scale = rows, vrows, roots[0]
        for i in range(1, 8):
            scale = jnp.where(sub == i, roots[i], scale)
        for j in range(7):
            c = jnp.zeros((8, 128), f32)
            for i in range(j + 1, 8):
                c = jnp.where(sub == i, w[i][j], c)
            new = new + c * full(rows[j : j + 1, :])
            vnew = vnew + c * full(vrows[j : j + 1, :])
        u_ref[8 * b : 8 * b + 8, :] = jnp.where(lane >= sub + 8 * b, new * scale, 0.0)
        w_ref[8 * b : 8 * b + 8, :] = vnew * scale
        if b == 15:
            break
        wi = [[w[t][j] * inv[t] for j in range(t)] for t in range(8)]
        brow = [full(new[t : t + 1, :]) for t in range(8)]
        bvrow = [full(vnew[t : t + 1, :]) for t in range(8)]
        for g in range(b + 1, 16):
            c = [full(s[g][:, 8 * b + j : 8 * b + j + 1]) for j in range(8)]
            for t in range(8):
                m = inv[t] * c[t]
                for j in range(t):
                    m = m + wi[t][j] * c[j]
                s[g] = s[g] - m * brow[t]
                v[g] = v[g] - m * bvrow[t]


def factor_kernel(index_ref, *refs):
    pieces, (l_ref, x_ref, a_ref, u_ref, w_ref) = refs[:8], refs[8:]
    for part, ref in enumerate(pieces):
        for n in range(4):
            j = index_ref[part * 4 + n]
            cols = pl.ds(pl.multiple_of(j % 4 * 256, 256), 256)
            for tile in range(8):
                rows = pl.ds(pl.multiple_of(tile * 128 + j // 4 * 16, 16), 16)
                a_ref[rows, cols] = ref[n, tile]
    l_ref[...] = jnp.zeros_like(l_ref)
    x_ref[...] = jnp.zeros_like(x_ref)
    for i in range(8):
        for j in range(i + 1):
            bi, bj = slice(128 * i, 128 * i + 128), slice(128 * j, 128 * j + 128)
            a_ref[bi, bj] = 0.5 * (a_ref[bi, bj] + a_ref[bj, bi].T)

    def step(b, carry):
        at = pl.ds(pl.multiple_of(b * 128, 128), 128)
        factor_block(a_ref[at, at], u_ref, w_ref)
        w = w_ref[...]
        l_ref[at, at] = u_ref[...].T
        x_ref[at, at] = w
        for n in range(8):

            @pl.when(b == n)
            def _():
                here = slice(128 * n, 128 * n + 128)
                if n < 7:
                    below = slice(128 * n + 128, PANEL)
                    low = times_transposed(a_ref[below, here], w)
                    l_ref[below, here] = low
                    for j in range(n + 1, 8):
                        rows, cols = slice(128 * j, PANEL), slice(128 * j, 128 * j + 128)
                        off = 128 * (j - n - 1)
                        a_ref[rows, cols] = a_ref[rows, cols] - times_transposed(
                            low[off:], low[off : off + 128]
                        )
                if n > 0:
                    done = slice(0, 128 * n)
                    x_ref[here, done] = -times(w, times(l_ref[here, done], x_ref[done, done]))

        return carry

    lax.fori_loop(0, 8, step, 0)


def factor(index, pieces):
    whole = pl.BlockSpec(memory_space=pltpu.VMEM)
    return pl.pallas_call(
        factor_kernel,
        in_specs=[pl.BlockSpec(memory_space=pltpu.SMEM)] + [whole] * 8,
        out_specs=[whole, whole],
        out_shape=[jax.ShapeDtypeStruct((PANEL, PANEL), f32)] * 2,
        scratch_shapes=[
            pltpu.VMEM((PANEL, PANEL), f32),
            pltpu.VMEM((128, 128), f32),
            pltpu.VMEM((128, 128), f32),
        ],
        compiler_params=pltpu.CompilerParams(vmem_limit_bytes=40 * MIB),
        cost_estimate=pl.CostEstimate(
            flops=7 * 10**10, bytes_accessed=12 * MIB, transcendentals=0
        ),
        name="factor_and_invert",
    )(index, *pieces)


def assemble_kernel(front_ref, got_ref, out_ref):
    for jc in range(4):
        cols = slice(jc * 256, jc * 256 + 256)
        out_ref[0, :, cols] = front_ref[0, 0, :, cols] + got_ref[:, jc, 0].reshape(128, 256)


def assemble(front, got):
    k = front.shape[0]
    return pl.pallas_call(
        assemble_kernel,
        grid=(k,),
        in_specs=[
            pl.BlockSpec((1, 1, 128, PANEL), lambda i: (i, 0, 0, 0)),
            pl.BlockSpec((8, 4, 1, 16, 256), lambda i: (0, 0, i, 0, 0)),
        ],
        out_specs=pl.BlockSpec((1, 128, PANEL), lambda i: (i, 0, 0)),
        out_shape=jax.ShapeDtypeStruct((k, 128, PANEL), f32),
        compiler_params=pltpu.CompilerParams(vmem_limit_bytes=56 * MIB),
        cost_estimate=pl.CostEstimate(
            flops=k * 128 * PANEL, bytes_accessed=12 * MIB, transcendentals=0
        ),
        name="assemble_panel",
    )(front, got)


def finish_kernel(order_ref, index_ref, panel_ref, lower_ref, top_ref, front_ref, got_ref, *refs):
    spread, pieces, (out_ref, slab_ref, rows_ref) = refs[:5], refs[5:13], refs[13:]
    step = pl.program_id(0)
    tiles = panel_ref.shape[0]
    leading = order_ref[4] == 0

    @pl.when(step == 0)
    def _():
        for part, ref in enumerate(pieces):
            for n in range(4):
                j = index_ref[part * 4 + n]
                for q in range(3):
                    at = (j % 4 * 3 + q) * 128 + j // 4 * 16
                    slab_ref[pl.ds(pl.multiple_of(at, 16), 16), :] = ref[n, q]

    for number in range(4):

        @pl.when(step == number)
        def _():
            if number == 2:
                rows_ref[:128, :] = spread[2][...]
                rows_ref[128:, :] = spread[3][...]
            else:
                rows_ref[...] = spread[number + number // 3][...]

    rows = rows_ref[...]

    @pl.when(leading)
    def _():
        out_ref[:, 0, :, :PANEL] = lower_ref[...]

    @pl.when(leading & (order_ref[step] == 0) & (order_ref[5] < 8))
    def _():
        out_ref[0, 0, :, :PANEL] = top_ref[...]

    @pl.when(jnp.logical_not(leading))
    def _():
        update = times_transposed(rows, slab_ref[:PANEL, :], None)
        out_ref[:, 0, :, :PANEL] = panel_ref[...] - update.reshape(tiles, 128, PANEL)

    update = times_transposed(rows, slab_ref[PANEL:, :], None).reshape(tiles, 128, -1)
    for jc in range(4):
        for tile in range(tiles):
            cols = slice(jc * 128, jc * 128 + 128)
            sums = got_ref[:, jc, tile].reshape(128, 128)
            out_ref[tile, 0, :, PANEL + jc * 128 : PANEL + jc * 128 + 128] = (
                front_ref[tile, 0, :, cols] + sums - update[tile, :, cols]
            )


def finish(order, index, panel, lower, top, front, got, spread, pieces):
    k, _, _, width = front.shape
    step = k // 4
    return pl.pallas_call(
        finish_kernel,
        grid_spec=pltpu.PrefetchScalarGridSpec(
            num_scalar_prefetch=2,
            grid=(4,),
            in_specs=[
                pl.BlockSpec((step, 128, PANEL), lambda i, o, _: (o[i], 0, 0)),
                pl.BlockSpec((step, 128, PANEL), lambda i, o, _: (o[i], 0, 0)),
                pl.BlockSpec((128, PANEL), lambda i, o, _: (0, 0)),
                pl.BlockSpec((step, 1, 128, 512), lambda i, o, _: (o[i], 0, 0, 2)),
                pl.BlockSpec((8, 4, step, 16, 128), lambda i, o, _: (0, 0, o[i], 0, 0)),
            ]
            + [pl.BlockSpec(x.shape, lambda i, o, _: (0, 0)) for x in spread]
            + [pl.BlockSpec(x.shape, lambda i, o, _: (0, 0, 0, 0)) for x in pieces],
            out_specs=pl.BlockSpec((step, 1, 128, width), lambda i, o, _: (o[i], 0, 0, 0)),
            scratch_shapes=[
                pltpu.VMEM((width, PANEL), bf16),
                pltpu.VMEM((step * 128, PANEL), bf16),
            ],
        ),
        out_shape=jax.ShapeDtypeStruct(front.shape, f32),
        compiler_params=pltpu.CompilerParams(vmem_limit_bytes=60 * MIB),
        cost_estimate=pl.CostEstimate(
            flops=2 * k * 128 * width * PANEL,
            bytes_accessed=28 * MIB,
            transcendentals=0,
        ),
        name="trailing_update",
    )(order, index, panel, lower, top, front, got, *spread, *pieces)


def exchange(x):
    return lax.all_to_all(x, "row", split_axis=0, concat_axis=0, tiled=True)


def row_number(x, z, core):
    return (x % 4 * 4 + z % 4) * 2 + core


def ring_stage(x, stage):
    parts = [x]
    for by in range(1, 4):
        moves = []
        for chip in range(16):
            for core in range(2):
                along_z = core == stage
                to = row_number(
                    chip // 4 + (0 if along_z else by), chip % 4 + (by if along_z else 0), core
                )
                moves.append((chip * 2 + core, to))
        parts.append(lax.ppermute(x, "row", moves))
    return parts


def gather_rows(ring):
    mine = ring_stage(ring, 1)
    return mine + [lax.ppermute(part, "row", [(r, r ^ 1) for r in range(32)]) for part in mine]


def gathered_index(row_index):
    number = jnp.arange(32, dtype=jnp.int32)
    half, outer, inner = number // 16, number // 4 % 4, number % 4
    core = (row_index + half) % 2
    chip = row_index // 2
    x = chip // 4 - jnp.where(core == 0, outer, inner) + 4
    z = chip % 4 - jnp.where(core == 0, inner, outer) + 4
    return row_number(x, z, core)


def from_first(pieces, col_index):
    result = jnp.where(col_index == 0, pieces[0], 0)
    for c in range(1, len(pieces)):
        result = result + lax.ppermute(pieces[c], "col", [(0, c)])
    return result


def own_rows(tiles, row_index):
    tiles = tiles.reshape(4, 3, 16, 256)
    quarter = row_index % 4
    result = jnp.zeros((3, 16, PANEL), f32)
    for by in range(4):
        part = lax.dynamic_index_in_dim(tiles, quarter ^ by, 0, keepdims=False)
        if by:
            part = lax.ppermute(part, "row", [(r, r ^ by) for r in range(32)])
        result = lax.dynamic_update_slice(result, part, (0, 0, (quarter ^ by) * 256))
    return result.reshape(48, PANEL)


def together(*arrays):
    return lax.optimization_barrier(arrays)


def body(front, child_tiles, tile_parent, tile_rows, tile_count):
    row_index = lax.axis_index("row").astype(jnp.int32)
    col_index = lax.axis_index("col").astype(jnp.int32)
    slots = child_tiles.shape[0]
    index = gathered_index(row_index)
    live = jnp.arange(slots, dtype=jnp.int32) < tile_count[0]
    rows = jnp.where(live[:, None], tile_rows, -1)
    at = (tile_parent % 32) * 8 + tile_parent // 32

    early = front[:2, 0, :, :PANEL].reshape(2, 8, 16, 4, 256).transpose(1, 3, 0, 2, 4)
    at = jnp.pad(at.astype(f32).reshape(1, slots), ((0, 7), (0, 256 - slots)))
    early = jnp.concatenate(
        [early.reshape(32, 32, 256), jnp.broadcast_to(at[None], (32, 8, 256))], axis=1
    )
    early = exchange(early)
    at = early[:, 32, :slots].astype(jnp.int32).reshape(32 * slots)
    early = early[:, :32].reshape(32, 2, 16, 256)

    sent = place(rows, child_tiles, 256, 0).reshape(32, slots, 16, 256)
    sent, early, at = together(sent, early, at)
    sent_rest = place(rows, child_tiles, 128, 2).reshape(32, slots, 16, 128)
    got, sent_rest = together(exchange(sent), sent_rest)
    sums = collect(at, got).reshape(32, 8, 16, 256)

    tiles = (sums[:, :2] + early).transpose(1, 0, 2, 3).reshape(64, 16, 256)
    pieces = [jnp.concatenate([tiles[:8], tiles[12 * c : 12 * c + 12]]) for c in range(4)]
    piece = from_first(pieces, col_index)
    ring, part = together(jnp.stack(ring_stage(piece[:8], 0)), own_rows(piece[8:], row_index))
    diagonal = gather_rows(ring)

    got, sent_rest = together(exchange(sums), sent_rest)
    panel = assemble(front, got.reshape(8, 4, 8, 16, 256))
    own = from_first([panel[2 * c : 2 * c + 2] for c in range(4)], col_index)
    got_rest = exchange(sent_rest)

    factored, inverse = factor(index, diagonal)

    def rows_of_factor(start, count):
        start = jnp.minimum(start, PANEL - count)
        return lax.dynamic_slice_in_dim(factored, start, count, 0)

    top = rows_of_factor(row_index * 128, 128)
    known, tile = [top], 12 * col_index + 3 * (row_index % 4)
    for q in range(3):
        known.append(rows_of_factor((tile + q) * 128 + row_index // 4 * 16, 16))
    known = jnp.concatenate(known)
    inside = jnp.concatenate(
        [
            jnp.broadcast_to((row_index < 8) & (col_index == 0), (128,)),
            jnp.repeat(tile + jnp.arange(3, dtype=jnp.int32) < 8, 16, total_repeat_length=48),
        ]
    )
    solved = jnp.concatenate([own.reshape(256, PANEL), part])
    solved = times_transposed(solved, inverse)
    both = jnp.concatenate([solved[:128], solved[256:]])
    both = jnp.where(inside[:, None], known, both).astype(bf16)
    own = jnp.concatenate([both[:128], solved[128:256].astype(bf16)])
    part = both[128:].reshape(3, 16, PANEL)

    def turn(x, by):
        return lax.ppermute(x, "col", [(c, (c + by) % 4) for c in range(4)])

    ring, before, behind = together(jnp.stack(ring_stage(part, 0)), turn(own, 1), turn(own, 3))
    spread = [own, before, turn(before[:128], 1), turn(behind[128:], 3), behind]
    slab = gather_rows(ring)

    sums_rest = collect(at, got_rest, own, part)
    got_rest = exchange(sums_rest.reshape(32, 8, 16, 128)).reshape(8, 4, 8, 16, 128)
    lower = times_transposed(panel.reshape(8 * 128, PANEL), inverse).reshape(8, 128, PANEL)

    order = (col_index + 4 - jnp.arange(4, dtype=jnp.int32)) % 4
    order = jnp.concatenate([order, jnp.stack([col_index, row_index])])
    return finish(order, index, panel, lower, top, front, got_rest, spread, slab)


def solution(mesh):
    placed = (
        P(None, "row", None, "col"),
        P("row", None, "col"),
        P("row"),
        P("row", None),
        P("row"),
    )
    return jax.shard_map(
        body, mesh=mesh, in_specs=placed, out_specs=P(None, "row", None, "col"), check_vma=False
    )
```

```python
import jax
import jax.numpy as jnp
from jax import lax
from jax.experimental import pallas as pl
from jax.experimental.pallas import tpu as pltpu
from jax.sharding import PartitionSpec as P

PANEL = 1024
HIGH = lax.Precision.HIGHEST
f32 = jnp.float32
bf16 = jnp.bfloat16
MIB = 2**20


def times_transposed(a, b, precision=HIGH):
    return lax.dot_general(
        a, b, (((1,), (1,)), ((), ())), precision=precision, preferred_element_type=f32
    )


def times(a, b):
    return lax.dot_general(
        a, b, (((1,), (0,)), ((), ())), precision=HIGH, preferred_element_type=f32
    )


def place_kernel(rows_ref, child_ref, out_ref):
    width = out_ref.shape[-1]
    position = lax.broadcasted_iota(jnp.int32, (128, 128), 0)
    for slot in range(4):
        hot = jnp.where(rows_ref[0, slot : slot + 1, :] == position, 1.0, 0.0).astype(bf16)
        placed = jnp.dot(hot, child_ref[slot], preferred_element_type=f32).astype(bf16)
        for jp in range(8):
            for jc in range(4):
                out_ref[jp, jc, slot] = placed[
                    jp * 16 : jp * 16 + 16, jc * width : jc * width + width
                ]


def place(rows, child_tiles, width, block):
    slots = child_tiles.shape[0]
    return pl.pallas_call(
        place_kernel,
        grid=(slots // 4,),
        in_specs=[
            pl.BlockSpec((1, 4, 128), lambda t: (t, 0, 0)),
            pl.BlockSpec((4, 128, 4 * width), lambda t: (t, 0, block)),
        ],
        out_specs=pl.BlockSpec((8, 4, 4, 16, width), lambda t: (0, 0, t, 0, 0)),
        out_shape=jax.ShapeDtypeStruct((8, 4, slots, 16, width), bf16),
        compiler_params=pltpu.CompilerParams(vmem_limit_bytes=56 * MIB),
        cost_estimate=pl.CostEstimate(
            flops=2 * slots * 128 * 128 * 4 * width,
            bytes_accessed=2 * slots * 128 * 4 * width * 2,
            transcendentals=0,
        ),
        name="place_rows",
    )(rows.reshape(slots // 4, 4, 128), child_tiles)


def collect_kernel(at_ref, got_ref, *refs):
    out_ref = refs[-1]
    step = pl.program_id(0)

    @pl.when(step == 0)
    def _():
        out_ref[...] = jnp.zeros_like(out_ref)

    sources, slots = got_ref.shape[:2]

    def add(source, carry):
        base = (step * sources + source) * slots
        for slot in range(slots):
            at = at_ref[base + slot]
            out_ref[at] = out_ref[at] + got_ref[source, slot].astype(f32)
        return carry

    lax.fori_loop(0, sources, add, 0)


def collect(at, got, *after):
    sources, slots, _, width = got.shape
    return pl.pallas_call(
        collect_kernel,
        grid_spec=pltpu.PrefetchScalarGridSpec(
            num_scalar_prefetch=1,
            grid=(sources // 4,),
            in_specs=[pl.BlockSpec((4, slots, 16, width), lambda s, at: (s, 0, 0, 0))]
            + [pl.BlockSpec(memory_space=pl.ANY)] * len(after),
            out_specs=pl.BlockSpec((256, 16, width), lambda s, at: (0, 0, 0)),
        ),
        out_shape=jax.ShapeDtypeStruct((256, 16, width), f32),
        compiler_params=pltpu.CompilerParams(vmem_limit_bytes=56 * MIB),
        cost_estimate=pl.CostEstimate(
            flops=sources * slots * 16 * width,
            bytes_accessed=sources * slots * 16 * width * 2 + 256 * 16 * width * 4,
            transcendentals=0,
        ),
        name="collect_parents",
    )(at, got, *after)


def factor_block(block, u_ref, w_ref):
    sub = lax.broadcasted_iota(jnp.int32, (8, 128), 0)
    lane = lax.broadcasted_iota(jnp.int32, (8, 128), 1)

    def full(x):
        return jnp.broadcast_to(x, (8, 128))

    s = [block[8 * g : 8 * g + 8, :] for g in range(16)]
    v = [jnp.where(lane == sub + 8 * g, 1.0, 0.0).astype(f32) for g in range(16)]
    for b in range(16):
        cols = [full(s[b][:, 8 * b + j : 8 * b + j + 1]) for j in range(8)]
        e = [[full(cols[j][i : i + 1, :]) for j in range(i + 1)] for i in range(8)]
        inv, w, roots = [], [], []
        f = [[None] * 8 for _ in range(8)]
        for t in range(8):
            pivot = e[t][t]
            inv.append(1.0 / pivot)
            root = lax.rsqrt(pivot)
            roots.append(root * (1.5 - 0.5 * pivot * root * root))
            for i in range(t + 1, 8):
                f[i][t] = e[i][t] * inv[t]
            for i in range(t + 1, 8):
                for j in range(t + 1, i + 1):
                    e[i][j] = e[i][j] - f[i][t] * e[j][t]
        for i in range(8):
            r = []
            for j in range(i):
                acc = f[i][j]
                for k in range(j + 1, i):
                    acc = acc + f[i][k] * w[k][j]
                r.append(-acc)
            w.append(r)
        rows, vrows = s[b], v[b]
        new, vnew, scale = rows, vrows, roots[0]
        for i in range(1, 8):
            scale = jnp.where(sub == i, roots[i], scale)
        for j in range(7):
            c = jnp.zeros((8, 128), f32)
            for i in range(j + 1, 8):
                c = jnp.where(sub == i, w[i][j], c)
            new = new + c * full(rows[j : j + 1, :])
            vnew = vnew + c * full(vrows[j : j + 1, :])
        u_ref[8 * b : 8 * b + 8, :] = jnp.where(lane >= sub + 8 * b, new * scale, 0.0)
        w_ref[8 * b : 8 * b + 8, :] = vnew * scale
        if b == 15:
            break
        wi = [[w[t][j] * inv[t] for j in range(t)] for t in range(8)]
        brow = [full(new[t : t + 1, :]) for t in range(8)]
        bvrow = [full(vnew[t : t + 1, :]) for t in range(8)]
        for g in range(b + 1, 16):
            c = [full(s[g][:, 8 * b + j : 8 * b + j + 1]) for j in range(8)]
            for t in range(8):
                m = inv[t] * c[t]
                for j in range(t):
                    m = m + wi[t][j] * c[j]
                s[g] = s[g] - m * brow[t]
                v[g] = v[g] - m * bvrow[t]


def factor_kernel(index_ref, *refs):
    pieces, (l_ref, x_ref, a_ref, u_ref, w_ref) = refs[:8], refs[8:]
    for part, ref in enumerate(pieces):
        for n in range(4):
            j = index_ref[part * 4 + n]
            cols = pl.ds(pl.multiple_of(j % 4 * 256, 256), 256)
            for tile in range(8):
                rows = pl.ds(pl.multiple_of(tile * 128 + j // 4 * 16, 16), 16)
                a_ref[rows, cols] = ref[n, tile]
    l_ref[...] = jnp.zeros_like(l_ref)
    x_ref[...] = jnp.zeros_like(x_ref)
    for i in range(8):
        for j in range(i + 1):
            bi, bj = slice(128 * i, 128 * i + 128), slice(128 * j, 128 * j + 128)
            a_ref[bi, bj] = 0.5 * (a_ref[bi, bj] + a_ref[bj, bi].T)

    def step(b, carry):
        at = pl.ds(pl.multiple_of(b * 128, 128), 128)
        factor_block(a_ref[at, at], u_ref, w_ref)
        w = w_ref[...]
        l_ref[at, at] = u_ref[...].T
        x_ref[at, at] = w
        for n in range(8):

            @pl.when(b == n)
            def _():
                here = slice(128 * n, 128 * n + 128)
                if n < 7:
                    below = slice(128 * n + 128, PANEL)
                    low = times_transposed(a_ref[below, here], w)
                    l_ref[below, here] = low
                    for j in range(n + 1, 8):
                        rows, cols = slice(128 * j, PANEL), slice(128 * j, 128 * j + 128)
                        off = 128 * (j - n - 1)
                        a_ref[rows, cols] = a_ref[rows, cols] - times_transposed(
                            low[off:], low[off : off + 128]
                        )
                if n > 0:
                    done = slice(0, 128 * n)
                    x_ref[here, done] = -times(w, times(l_ref[here, done], x_ref[done, done]))

        return carry

    lax.fori_loop(0, 8, step, 0)


def factor(index, pieces):
    whole = pl.BlockSpec(memory_space=pltpu.VMEM)
    return pl.pallas_call(
        factor_kernel,
        in_specs=[pl.BlockSpec(memory_space=pltpu.SMEM)] + [whole] * 8,
        out_specs=[whole, whole],
        out_shape=[jax.ShapeDtypeStruct((PANEL, PANEL), f32)] * 2,
        scratch_shapes=[
            pltpu.VMEM((PANEL, PANEL), f32),
            pltpu.VMEM((128, 128), f32),
            pltpu.VMEM((128, 128), f32),
        ],
        compiler_params=pltpu.CompilerParams(vmem_limit_bytes=40 * MIB),
        cost_estimate=pl.CostEstimate(
            flops=7 * 10**10, bytes_accessed=12 * MIB, transcendentals=0
        ),
        name="factor_and_invert",
    )(index, *pieces)


def assemble_kernel(front_ref, got_ref, out_ref):
    for jc in range(4):
        cols = slice(jc * 256, jc * 256 + 256)
        out_ref[0, :, cols] = front_ref[0, 0, :, cols] + got_ref[:, jc, 0].reshape(128, 256)


def assemble(front, got):
    k = front.shape[0]
    return pl.pallas_call(
        assemble_kernel,
        grid=(k,),
        in_specs=[
            pl.BlockSpec((1, 1, 128, PANEL), lambda i: (i, 0, 0, 0)),
            pl.BlockSpec((8, 4, 1, 16, 256), lambda i: (0, 0, i, 0, 0)),
        ],
        out_specs=pl.BlockSpec((1, 128, PANEL), lambda i: (i, 0, 0)),
        out_shape=jax.ShapeDtypeStruct((k, 128, PANEL), f32),
        compiler_params=pltpu.CompilerParams(vmem_limit_bytes=56 * MIB),
        cost_estimate=pl.CostEstimate(
            flops=k * 128 * PANEL, bytes_accessed=12 * MIB, transcendentals=0
        ),
        name="assemble_panel",
    )(front, got)


def finish_kernel(order_ref, index_ref, panel_ref, lower_ref, top_ref, front_ref, got_ref, *refs):
    spread, pieces, (out_ref, slab_ref, rows_ref) = refs[:5], refs[5:13], refs[13:]
    step = pl.program_id(0)
    tiles = panel_ref.shape[0]
    leading = order_ref[4] == 0

    @pl.when(step == 0)
    def _():
        for part, ref in enumerate(pieces):
            for n in range(4):
                j = index_ref[part * 4 + n]
                for q in range(3):
                    at = (j % 4 * 3 + q) * 128 + j // 4 * 16
                    slab_ref[pl.ds(pl.multiple_of(at, 16), 16), :] = ref[n, q]

    for number in range(4):

        @pl.when(step == number)
        def _():
            if number == 2:
                rows_ref[:128, :] = spread[2][...]
                rows_ref[128:, :] = spread[3][...]
            else:
                rows_ref[...] = spread[number + number // 3][...]

    rows = rows_ref[...]

    @pl.when(leading)
    def _():
        out_ref[:, 0, :, :PANEL] = lower_ref[...]

    @pl.when(leading & (order_ref[step] == 0) & (order_ref[5] < 8))
    def _():
        out_ref[0, 0, :, :PANEL] = top_ref[...]

    @pl.when(jnp.logical_not(leading))
    def _():
        update = times_transposed(rows, slab_ref[:PANEL, :], None)
        out_ref[:, 0, :, :PANEL] = panel_ref[...] - update.reshape(tiles, 128, PANEL)

    update = times_transposed(rows, slab_ref[PANEL:, :], None).reshape(tiles, 128, -1)
    for jc in range(4):
        for tile in range(tiles):
            cols = slice(jc * 128, jc * 128 + 128)
            sums = got_ref[:, jc, tile].reshape(128, 128)
            out_ref[tile, 0, :, PANEL + jc * 128 : PANEL + jc * 128 + 128] = (
                front_ref[tile, 0, :, cols] + sums - update[tile, :, cols]
            )


def finish(order, index, panel, lower, top, front, got, spread, pieces):
    k, _, _, width = front.shape
    step = k // 4
    return pl.pallas_call(
        finish_kernel,
        grid_spec=pltpu.PrefetchScalarGridSpec(
            num_scalar_prefetch=2,
            grid=(4,),
            in_specs=[
                pl.BlockSpec((step, 128, PANEL), lambda i, o, _: (o[i], 0, 0)),
                pl.BlockSpec((step, 128, PANEL), lambda i, o, _: (o[i], 0, 0)),
                pl.BlockSpec((128, PANEL), lambda i, o, _: (0, 0)),
                pl.BlockSpec((step, 1, 128, 512), lambda i, o, _: (o[i], 0, 0, 2)),
                pl.BlockSpec((8, 4, step, 16, 128), lambda i, o, _: (0, 0, o[i], 0, 0)),
            ]
            + [pl.BlockSpec(x.shape, lambda i, o, _: (0, 0)) for x in spread]
            + [pl.BlockSpec(x.shape, lambda i, o, _: (0, 0, 0, 0)) for x in pieces],
            out_specs=pl.BlockSpec((step, 1, 128, width), lambda i, o, _: (o[i], 0, 0, 0)),
            scratch_shapes=[
                pltpu.VMEM((width, PANEL), bf16),
                pltpu.VMEM((step * 128, PANEL), bf16),
            ],
        ),
        out_shape=jax.ShapeDtypeStruct(front.shape, f32),
        compiler_params=pltpu.CompilerParams(vmem_limit_bytes=60 * MIB),
        cost_estimate=pl.CostEstimate(
            flops=2 * k * 128 * width * PANEL,
            bytes_accessed=28 * MIB,
            transcendentals=0,
        ),
        name="trailing_update",
    )(order, index, panel, lower, top, front, got, *spread, *pieces)


def exchange(x):
    return lax.all_to_all(x, "row", split_axis=0, concat_axis=0, tiled=True)


def row_number(x, z, core):
    return (x % 4 * 4 + z % 4) * 2 + core


def ring_stage(x, stage):
    parts = [x]
    for by in range(1, 4):
        moves = []
        for chip in range(16):
            for core in range(2):
                along_z = core == stage
                to = row_number(
                    chip // 4 + (0 if along_z else by), chip % 4 + (by if along_z else 0), core
                )
                moves.append((chip * 2 + core, to))
        parts.append(lax.ppermute(x, "row", moves))
    return parts


def with_cores(mine):
    return mine + [lax.ppermute(part, "row", [(r, r ^ 1) for r in range(32)]) for part in mine]


def gathered_index(row_index):
    number = jnp.arange(32, dtype=jnp.int32)
    half, outer, inner = number // 16, number // 4 % 4, number % 4
    core = (row_index + half) % 2
    chip = row_index // 2
    x = chip // 4 - jnp.where(core == 0, outer, inner) + 4
    z = chip % 4 - jnp.where(core == 0, inner, outer) + 4
    return row_number(x, z, core)


def from_first(pieces, col_index):
    result = jnp.where(col_index == 0, pieces[0], 0)
    for c in range(1, len(pieces)):
        result = result + lax.ppermute(pieces[c], "col", [(0, c)])
    return result


def own_rows(tiles, row_index):
    tiles = tiles.reshape(4, 3, 16, 256)
    quarter = row_index % 4
    result = jnp.zeros((3, 16, PANEL), f32)
    for by in range(4):
        part = lax.dynamic_index_in_dim(tiles, quarter ^ by, 0, keepdims=False)
        if by:
            part = lax.ppermute(part, "row", [(r, r ^ by) for r in range(32)])
        result = lax.dynamic_update_slice(result, part, (0, 0, (quarter ^ by) * 256))
    return result.reshape(48, PANEL)


def together(*arrays):
    return lax.optimization_barrier(arrays)


def body(front, child_tiles, tile_parent, tile_rows, tile_count):
    row_index = lax.axis_index("row").astype(jnp.int32)
    col_index = lax.axis_index("col").astype(jnp.int32)
    slots = child_tiles.shape[0]
    index = gathered_index(row_index)
    live = jnp.arange(slots, dtype=jnp.int32) < tile_count[0]
    rows = jnp.where(live[:, None], tile_rows, -1)
    at = (tile_parent % 32) * 8 + tile_parent // 32

    early = front[:2, 0, :, :PANEL].reshape(2, 8, 16, 4, 256).transpose(1, 3, 0, 2, 4)
    at = jnp.pad(at.astype(f32).reshape(1, slots), ((0, 7), (0, 256 - slots)))
    early = jnp.concatenate(
        [early.reshape(32, 32, 256), jnp.broadcast_to(at[None], (32, 8, 256))], axis=1
    )
    early = exchange(early)
    at = early[:, 32, :slots].astype(jnp.int32).reshape(32 * slots)
    early = early[:, :32].reshape(32, 2, 16, 256)

    sent = place(rows, child_tiles, 256, 0).reshape(32, slots, 16, 256)
    sent, early, at = together(sent, early, at)
    sent_rest = place(rows, child_tiles, 128, 2).reshape(32, slots, 16, 128)
    got, sent_rest = together(exchange(sent), sent_rest)
    sums = collect(at, got).reshape(32, 8, 16, 256)

    tiles = (sums[:, :2] + early).transpose(1, 0, 2, 3).reshape(64, 16, 256)
    pieces = [jnp.concatenate([tiles[:8], tiles[12 * c : 12 * c + 12]]) for c in range(4)]
    piece = from_first(pieces, col_index)
    ring, part = together(jnp.stack(ring_stage(piece[:8], 0)), own_rows(piece[8:], row_index))
    diagonal = with_cores(ring_stage(ring, 1))

    got, sent_rest = together(exchange(sums), sent_rest)
    panel = assemble(front, got.reshape(8, 4, 8, 16, 256))
    own = from_first([panel[2 * c : 2 * c + 2] for c in range(4)], col_index)
    got_rest = exchange(sent_rest)

    factored, inverse = factor(index, diagonal)

    def rows_of_factor(start, count):
        start = jnp.minimum(start, PANEL - count)
        return lax.dynamic_slice_in_dim(factored, start, count, 0)

    top = rows_of_factor(row_index * 128, 128)
    known, tile = [top], 12 * col_index + 3 * (row_index % 4)
    for q in range(3):
        known.append(rows_of_factor((tile + q) * 128 + row_index // 4 * 16, 16))
    known = jnp.concatenate(known)
    inside = jnp.concatenate(
        [
            jnp.broadcast_to((row_index < 8) & (col_index == 0), (128,)),
            jnp.repeat(tile + jnp.arange(3, dtype=jnp.int32) < 8, 16, total_repeat_length=48),
        ]
    )
    solved = jnp.concatenate([own.reshape(256, PANEL), part])
    solved = times_transposed(solved, inverse)
    both = jnp.concatenate([solved[:128], solved[256:]])
    both = jnp.where(inside[:, None], known, both).astype(bf16)
    own = jnp.concatenate([both[:128], solved[128:256].astype(bf16)])
    part = both[128:].reshape(3, 16, PANEL)

    def turn(x, by):
        return lax.ppermute(x, "col", [(c, (c + by) % 4) for c in range(4)])

    before, behind = turn(own, 1), turn(own, 3)
    sums_rest = collect(at, got_rest, own, part)
    ring, sums_rest = together(jnp.stack(ring_stage(part, 0)), sums_rest)
    got_rest = exchange(sums_rest.reshape(32, 8, 16, 128)).reshape(8, 4, 8, 16, 128)
    lower = times_transposed(panel.reshape(8 * 128, PANEL), inverse).reshape(8, 128, PANEL)
    *mine, lower, before, behind = together(*ring_stage(ring, 1), lower, before, behind)
    spread = [own, before, turn(before[:128], 1), turn(behind[128:], 3), behind]
    slab = with_cores(mine)

    order = (col_index + 4 - jnp.arange(4, dtype=jnp.int32)) % 4
    order = jnp.concatenate([order, jnp.stack([col_index, row_index])])
    return finish(order, index, panel, lower, top, front, got_rest, spread, slab)


def solution(mesh):
    placed = (
        P(None, "row", None, "col"),
        P("row", None, "col"),
        P("row"),
        P("row", None),
        P("row"),
    )
    return jax.shard_map(
        body, mesh=mesh, in_specs=placed, out_specs=P(None, "row", None, "col"), check_vma=False
    )
```

```python
import jax
import jax.numpy as jnp
from jax import lax
from jax.experimental import pallas as pl
from jax.experimental.pallas import tpu as pltpu
from jax.sharding import PartitionSpec as P

PANEL = 1024
HIGH = lax.Precision.HIGHEST
f32 = jnp.float32
bf16 = jnp.bfloat16
MIB = 2**20


def times_transposed(a, b, precision=HIGH):
    return lax.dot_general(
        a, b, (((1,), (1,)), ((), ())), precision=precision, preferred_element_type=f32
    )


def times(a, b):
    return lax.dot_general(
        a, b, (((1,), (0,)), ((), ())), precision=HIGH, preferred_element_type=f32
    )


def place_kernel(rows_ref, child_ref, out_ref):
    width = out_ref.shape[-1]
    position = lax.broadcasted_iota(jnp.int32, (128, 128), 0)
    for slot in range(4):
        hot = jnp.where(rows_ref[0, slot : slot + 1, :] == position, 1.0, 0.0).astype(bf16)
        placed = jnp.dot(hot, child_ref[slot], preferred_element_type=f32).astype(bf16)
        for jp in range(8):
            for jc in range(4):
                out_ref[jp, jc, slot] = placed[
                    jp * 16 : jp * 16 + 16, jc * width : jc * width + width
                ]


def place(rows, child_tiles, width, block):
    slots = child_tiles.shape[0]
    return pl.pallas_call(
        place_kernel,
        grid=(slots // 4,),
        in_specs=[
            pl.BlockSpec((1, 4, 128), lambda t: (t, 0, 0)),
            pl.BlockSpec((4, 128, 4 * width), lambda t: (t, 0, block)),
        ],
        out_specs=pl.BlockSpec((8, 4, 4, 16, width), lambda t: (0, 0, t, 0, 0)),
        out_shape=jax.ShapeDtypeStruct((8, 4, slots, 16, width), bf16),
        compiler_params=pltpu.CompilerParams(vmem_limit_bytes=56 * MIB),
        cost_estimate=pl.CostEstimate(
            flops=2 * slots * 128 * 128 * 4 * width,
            bytes_accessed=2 * slots * 128 * 4 * width * 2,
            transcendentals=0,
        ),
        name="place_rows",
    )(rows.reshape(slots // 4, 4, 128), child_tiles)


def collect_kernel(at_ref, got_ref, *refs):
    out_ref, odd_ref = refs[-2:]
    step = pl.program_id(0)

    @pl.when(step == 0)
    def _():
        out_ref[...] = jnp.zeros_like(out_ref)
        odd_ref[...] = jnp.zeros_like(odd_ref)

    sources, slots = got_ref.shape[:2]

    def add(pair, carry):
        source = pair * 2
        base = (step * sources + source) * slots
        for slot in range(slots):
            at, odd = at_ref[base + slot], at_ref[base + slots + slot]
            out_ref[at] = out_ref[at] + got_ref[source, slot].astype(f32)
            odd_ref[odd] = odd_ref[odd] + got_ref[source + 1, slot].astype(f32)
        return carry

    lax.fori_loop(0, sources // 2, add, 0)

    @pl.when(step == pl.num_programs(0) - 1)
    def _():
        out_ref[...] = out_ref[...] + odd_ref[...]


def collect(at, got, *after):
    sources, slots, _, width = got.shape
    return pl.pallas_call(
        collect_kernel,
        grid_spec=pltpu.PrefetchScalarGridSpec(
            num_scalar_prefetch=1,
            grid=(sources // 4,),
            in_specs=[pl.BlockSpec((4, slots, 16, width), lambda s, at: (s, 0, 0, 0))]
            + [pl.BlockSpec(memory_space=pl.ANY)] * len(after),
            out_specs=pl.BlockSpec((256, 16, width), lambda s, at: (0, 0, 0)),
            scratch_shapes=[pltpu.VMEM((256, 16, width), f32)],
        ),
        out_shape=jax.ShapeDtypeStruct((256, 16, width), f32),
        compiler_params=pltpu.CompilerParams(vmem_limit_bytes=56 * MIB),
        cost_estimate=pl.CostEstimate(
            flops=sources * slots * 16 * width,
            bytes_accessed=sources * slots * 16 * width * 2 + 256 * 16 * width * 4,
            transcendentals=0,
        ),
        name="collect_parents",
    )(at, got, *after)


def factor_block(block, u_ref, w_ref):
    sub = lax.broadcasted_iota(jnp.int32, (8, 128), 0)
    lane = lax.broadcasted_iota(jnp.int32, (8, 128), 1)

    def full(x):
        return jnp.broadcast_to(x, (8, 128))

    s = [block[8 * g : 8 * g + 8, :] for g in range(16)]
    v = [jnp.where(lane == sub + 8 * g, 1.0, 0.0).astype(f32) for g in range(16)]
    for b in range(16):
        cols = [full(s[b][:, 8 * b + j : 8 * b + j + 1]) for j in range(8)]
        e = [[full(cols[j][i : i + 1, :]) for j in range(i + 1)] for i in range(8)]
        inv, w, roots = [], [], []
        f = [[None] * 8 for _ in range(8)]
        for t in range(8):
            pivot = e[t][t]
            inv.append(1.0 / pivot)
            root = lax.rsqrt(pivot)
            roots.append(root * (1.5 - 0.5 * pivot * root * root))
            for i in range(t + 1, 8):
                f[i][t] = e[i][t] * inv[t]
            for i in range(t + 1, 8):
                for j in range(t + 1, i + 1):
                    e[i][j] = e[i][j] - f[i][t] * e[j][t]
        for i in range(8):
            r = []
            for j in range(i):
                acc = f[i][j]
                for k in range(j + 1, i):
                    acc = acc + f[i][k] * w[k][j]
                r.append(-acc)
            w.append(r)
        rows, vrows = s[b], v[b]
        new, vnew, scale = rows, vrows, roots[0]
        for i in range(1, 8):
            scale = jnp.where(sub == i, roots[i], scale)
        for j in range(7):
            c = jnp.zeros((8, 128), f32)
            for i in range(j + 1, 8):
                c = jnp.where(sub == i, w[i][j], c)
            new = new + c * full(rows[j : j + 1, :])
            vnew = vnew + c * full(vrows[j : j + 1, :])
        u_ref[8 * b : 8 * b + 8, :] = jnp.where(lane >= sub + 8 * b, new * scale, 0.0)
        w_ref[8 * b : 8 * b + 8, :] = vnew * scale
        if b == 15:
            break
        wi = [[w[t][j] * inv[t] for j in range(t)] for t in range(8)]
        brow = [full(new[t : t + 1, :]) for t in range(8)]
        bvrow = [full(vnew[t : t + 1, :]) for t in range(8)]
        for g in range(b + 1, 16):
            c = [full(s[g][:, 8 * b + j : 8 * b + j + 1]) for j in range(8)]
            for t in range(8):
                m = inv[t] * c[t]
                for j in range(t):
                    m = m + wi[t][j] * c[j]
                s[g] = s[g] - m * brow[t]
                v[g] = v[g] - m * bvrow[t]


def factor_kernel(index_ref, *refs):
    pieces, (l_ref, x_ref, a_ref, u_ref, w_ref) = refs[:8], refs[8:]
    for part, ref in enumerate(pieces):
        for n in range(4):
            j = index_ref[part * 4 + n]
            cols = pl.ds(pl.multiple_of(j % 4 * 256, 256), 256)
            for tile in range(8):
                rows = pl.ds(pl.multiple_of(tile * 128 + j // 4 * 16, 16), 16)
                a_ref[rows, cols] = ref[n, tile]
    l_ref[...] = jnp.zeros_like(l_ref)
    x_ref[...] = jnp.zeros_like(x_ref)
    for i in range(8):
        for j in range(i + 1):
            bi, bj = slice(128 * i, 128 * i + 128), slice(128 * j, 128 * j + 128)
            a_ref[bi, bj] = 0.5 * (a_ref[bi, bj] + a_ref[bj, bi].T)

    def step(b, carry):
        at = pl.ds(pl.multiple_of(b * 128, 128), 128)
        factor_block(a_ref[at, at], u_ref, w_ref)
        w = w_ref[...]
        l_ref[at, at] = u_ref[...].T
        x_ref[at, at] = w
        for n in range(8):

            @pl.when(b == n)
            def _():
                here = slice(128 * n, 128 * n + 128)
                if n < 7:
                    below = slice(128 * n + 128, PANEL)
                    low = times_transposed(a_ref[below, here], w)
                    l_ref[below, here] = low
                    for j in range(n + 1, 8):
                        rows, cols = slice(128 * j, PANEL), slice(128 * j, 128 * j + 128)
                        off = 128 * (j - n - 1)
                        a_ref[rows, cols] = a_ref[rows, cols] - times_transposed(
                            low[off:], low[off : off + 128]
                        )
                if n > 0:
                    done = slice(0, 128 * n)
                    x_ref[here, done] = -times(w, times(l_ref[here, done], x_ref[done, done]))

        return carry

    lax.fori_loop(0, 8, step, 0)


def factor(index, pieces):
    whole = pl.BlockSpec(memory_space=pltpu.VMEM)
    return pl.pallas_call(
        factor_kernel,
        in_specs=[pl.BlockSpec(memory_space=pltpu.SMEM)] + [whole] * 8,
        out_specs=[whole, whole],
        out_shape=[jax.ShapeDtypeStruct((PANEL, PANEL), f32)] * 2,
        scratch_shapes=[
            pltpu.VMEM((PANEL, PANEL), f32),
            pltpu.VMEM((128, 128), f32),
            pltpu.VMEM((128, 128), f32),
        ],
        compiler_params=pltpu.CompilerParams(vmem_limit_bytes=40 * MIB),
        cost_estimate=pl.CostEstimate(
            flops=7 * 10**10, bytes_accessed=12 * MIB, transcendentals=0
        ),
        name="factor_and_invert",
    )(index, *pieces)


def assemble_kernel(front_ref, got_ref, out_ref):
    for tile in range(2):
        for jc in range(4):
            cols = slice(jc * 256, jc * 256 + 256)
            sums = got_ref[:, jc, tile].reshape(128, 256)
            out_ref[tile, :, cols] = front_ref[tile, 0, :, cols] + sums


def assemble(front, got):
    k = front.shape[0]
    return pl.pallas_call(
        assemble_kernel,
        grid=(k // 2,),
        in_specs=[
            pl.BlockSpec((2, 1, 128, PANEL), lambda i: (i, 0, 0, 0)),
            pl.BlockSpec((8, 4, 2, 16, 256), lambda i: (0, 0, i, 0, 0)),
        ],
        out_specs=pl.BlockSpec((2, 128, PANEL), lambda i: (i, 0, 0)),
        out_shape=jax.ShapeDtypeStruct((k, 128, PANEL), f32),
        compiler_params=pltpu.CompilerParams(vmem_limit_bytes=56 * MIB),
        cost_estimate=pl.CostEstimate(
            flops=k * 128 * PANEL, bytes_accessed=12 * MIB, transcendentals=0
        ),
        name="assemble_panel",
    )(front, got)


def finish_kernel(order_ref, index_ref, panel_ref, lower_ref, top_ref, front_ref, got_ref, *refs):
    spread, pieces, (out_ref, slab_ref, rows_ref) = refs[:5], refs[5:13], refs[13:]
    step = pl.program_id(0)
    tiles = panel_ref.shape[0]
    leading = order_ref[4] == 0

    @pl.when(step == 0)
    def _():
        for part, ref in enumerate(pieces):
            for n in range(4):
                j = index_ref[part * 4 + n]
                for q in range(3):
                    at = (j % 4 * 3 + q) * 128 + j // 4 * 16
                    slab_ref[pl.ds(pl.multiple_of(at, 16), 16), :] = ref[n, q]

    for number in range(4):

        @pl.when(step == number)
        def _():
            if number == 2:
                rows_ref[:128, :] = spread[2][...]
                rows_ref[128:, :] = spread[3][...]
            else:
                rows_ref[...] = spread[number + number // 3][...]

    rows = rows_ref[...]

    @pl.when(leading)
    def _():
        out_ref[:, 0, :, :PANEL] = lower_ref[...]

    @pl.when(leading & (order_ref[step] == 0) & (order_ref[5] < 8))
    def _():
        out_ref[0, 0, :, :PANEL] = top_ref[...]

    @pl.when(jnp.logical_not(leading))
    def _():
        update = times_transposed(rows, slab_ref[:PANEL, :], None)
        out_ref[:, 0, :, :PANEL] = panel_ref[...] - update.reshape(tiles, 128, PANEL)

    update = times_transposed(rows, slab_ref[PANEL:, :], None).reshape(tiles, 128, -1)
    for jc in range(4):
        for tile in range(tiles):
            cols = slice(jc * 128, jc * 128 + 128)
            sums = got_ref[:, jc, tile].reshape(128, 128)
            out_ref[tile, 0, :, PANEL + jc * 128 : PANEL + jc * 128 + 128] = (
                front_ref[tile, 0, :, cols] + sums - update[tile, :, cols]
            )


def finish(order, index, panel, lower, top, front, got, spread, pieces):
    k, _, _, width = front.shape
    step = k // 4
    return pl.pallas_call(
        finish_kernel,
        grid_spec=pltpu.PrefetchScalarGridSpec(
            num_scalar_prefetch=2,
            grid=(4,),
            in_specs=[
                pl.BlockSpec((step, 128, PANEL), lambda i, o, _: (o[i], 0, 0)),
                pl.BlockSpec((step, 128, PANEL), lambda i, o, _: (o[i], 0, 0)),
                pl.BlockSpec((128, PANEL), lambda i, o, _: (0, 0)),
                pl.BlockSpec((step, 1, 128, 512), lambda i, o, _: (o[i], 0, 0, 2)),
                pl.BlockSpec((8, 4, step, 16, 128), lambda i, o, _: (0, 0, o[i], 0, 0)),
            ]
            + [pl.BlockSpec(x.shape, lambda i, o, _: (0, 0)) for x in spread]
            + [pl.BlockSpec(x.shape, lambda i, o, _: (0, 0, 0, 0)) for x in pieces],
            out_specs=pl.BlockSpec((step, 1, 128, width), lambda i, o, _: (o[i], 0, 0, 0)),
            scratch_shapes=[
                pltpu.VMEM((width, PANEL), bf16),
                pltpu.VMEM((step * 128, PANEL), bf16),
            ],
        ),
        out_shape=jax.ShapeDtypeStruct(front.shape, f32),
        compiler_params=pltpu.CompilerParams(vmem_limit_bytes=60 * MIB),
        cost_estimate=pl.CostEstimate(
            flops=2 * k * 128 * width * PANEL,
            bytes_accessed=28 * MIB,
            transcendentals=0,
        ),
        name="trailing_update",
    )(order, index, panel, lower, top, front, got, *spread, *pieces)


def exchange(x):
    return lax.all_to_all(x, "row", split_axis=0, concat_axis=0, tiled=True)


def row_number(x, z, core):
    return (x % 4 * 4 + z % 4) * 2 + core


def ring_stage(x, stage):
    parts = [x]
    for by in range(1, 4):
        moves = []
        for chip in range(16):
            for core in range(2):
                along_z = core == stage
                to = row_number(
                    chip // 4 + (0 if along_z else by), chip % 4 + (by if along_z else 0), core
                )
                moves.append((chip * 2 + core, to))
        parts.append(lax.ppermute(x, "row", moves))
    return parts


def with_cores(mine):
    return mine + [lax.ppermute(part, "row", [(r, r ^ 1) for r in range(32)]) for part in mine]


def gathered_index(row_index):
    number = jnp.arange(32, dtype=jnp.int32)
    half, outer, inner = number // 16, number // 4 % 4, number % 4
    core = (row_index + half) % 2
    chip = row_index // 2
    x = chip // 4 - jnp.where(core == 0, outer, inner) + 4
    z = chip % 4 - jnp.where(core == 0, inner, outer) + 4
    return row_number(x, z, core)


def from_first(pieces, col_index):
    result = jnp.where(col_index == 0, pieces[0], 0)
    for c in range(1, len(pieces)):
        result = result + lax.ppermute(pieces[c], "col", [(0, c)])
    return result


def own_rows(tiles, row_index):
    tiles = tiles.reshape(4, 3, 16, 256)
    quarter = row_index % 4
    result = jnp.zeros((3, 16, PANEL), f32)
    for by in range(4):
        part = lax.dynamic_index_in_dim(tiles, quarter ^ by, 0, keepdims=False)
        if by:
            part = lax.ppermute(part, "row", [(r, r ^ by) for r in range(32)])
        result = lax.dynamic_update_slice(result, part, (0, 0, (quarter ^ by) * 256))
    return result.reshape(48, PANEL)


def together(*arrays):
    return lax.optimization_barrier(arrays)


def body(front, child_tiles, tile_parent, tile_rows, tile_count):
    row_index = lax.axis_index("row").astype(jnp.int32)
    col_index = lax.axis_index("col").astype(jnp.int32)
    slots = child_tiles.shape[0]
    index = gathered_index(row_index)
    live = jnp.arange(slots, dtype=jnp.int32) < tile_count[0]
    rows = jnp.where(live[:, None], tile_rows, -1)
    at = (tile_parent % 32) * 8 + tile_parent // 32

    early = front[:2, 0, :, :PANEL].reshape(2, 8, 16, 4, 256).transpose(1, 3, 0, 2, 4)
    at = jnp.pad(at.astype(f32).reshape(1, slots), ((0, 7), (0, 256 - slots)))
    early = jnp.concatenate(
        [early.reshape(32, 32, 256), jnp.broadcast_to(at[None], (32, 8, 256))], axis=1
    )
    early = exchange(early)
    at = early[:, 32, :slots].astype(jnp.int32).reshape(32 * slots)
    early = early[:, :32].reshape(32, 2, 16, 256)

    sent = place(rows, child_tiles, 256, 0).reshape(32, slots, 16, 256)
    sent, early, at = together(sent, early, at)
    sent_rest = place(rows, child_tiles, 128, 2).reshape(32, slots, 16, 128)
    got, sent_rest = together(exchange(sent), sent_rest)
    sums = collect(at, got).reshape(32, 8, 16, 256)

    tiles = (sums[:, :2] + early).transpose(1, 0, 2, 3).reshape(64, 16, 256)
    pieces = [jnp.concatenate([tiles[:8], tiles[12 * c : 12 * c + 12]]) for c in range(4)]
    piece = from_first(pieces, col_index)
    ring, part = together(jnp.stack(ring_stage(piece[:8], 0)), own_rows(piece[8:], row_index))
    diagonal = with_cores(ring_stage(ring, 1))

    got, sent_rest = together(exchange(sums), sent_rest)
    panel = assemble(front, got.reshape(8, 4, 8, 16, 256))
    own = from_first([panel[2 * c : 2 * c + 2] for c in range(4)], col_index)
    got_rest = exchange(sent_rest)

    factored, inverse = factor(index, diagonal)

    def rows_of_factor(start, count):
        start = jnp.minimum(start, PANEL - count)
        return lax.dynamic_slice_in_dim(factored, start, count, 0)

    top = rows_of_factor(row_index * 128, 128)
    known, tile = [top], 12 * col_index + 3 * (row_index % 4)
    for q in range(3):
        known.append(rows_of_factor((tile + q) * 128 + row_index // 4 * 16, 16))
    known = jnp.concatenate(known)
    inside = jnp.concatenate(
        [
            jnp.broadcast_to((row_index < 8) & (col_index == 0), (128,)),
            jnp.repeat(tile + jnp.arange(3, dtype=jnp.int32) < 8, 16, total_repeat_length=48),
        ]
    )
    solved = jnp.concatenate([own.reshape(256, PANEL), part])
    solved = times_transposed(solved, inverse)
    both = jnp.concatenate([solved[:128], solved[256:]])
    both = jnp.where(inside[:, None], known, both).astype(bf16)
    own = jnp.concatenate([both[:128], solved[128:256].astype(bf16)])
    part = both[128:].reshape(3, 16, PANEL)

    def turn(x, by):
        return lax.ppermute(x, "col", [(c, (c + by) % 4) for c in range(4)])

    before, behind = turn(own, 1), turn(own, 3)
    sums_rest = collect(at, got_rest, own, part)
    ring, sums_rest, before, behind = together(
        jnp.stack(ring_stage(part, 0)), sums_rest, before, behind
    )
    got_rest = exchange(sums_rest.reshape(32, 8, 16, 128)).reshape(8, 4, 8, 16, 128)
    lower = times_transposed(panel.reshape(8 * 128, PANEL), inverse).reshape(8, 128, PANEL)
    far = turn(before[:128], 1), turn(behind[128:], 3)
    *mine, lower, far_before, far_behind = together(*ring_stage(ring, 1), lower, *far)
    spread = [own, before, far_before, far_behind, behind]
    slab = with_cores(mine)

    order = (col_index + 4 - jnp.arange(4, dtype=jnp.int32)) % 4
    order = jnp.concatenate([order, jnp.stack([col_index, row_index])])
    return finish(order, index, panel, lower, top, front, got_rest, spread, slab)


def solution(mesh):
    placed = (
        P(None, "row", None, "col"),
        P("row", None, "col"),
        P("row"),
        P("row", None),
        P("row"),
    )
    return jax.shard_map(
        body, mesh=mesh, in_specs=placed, out_specs=P(None, "row", None, "col"), check_vma=False
    )
```

```python
import jax
import jax.numpy as jnp
from jax import lax
from jax.experimental import pallas as pl
from jax.experimental.pallas import tpu as pltpu
from jax.sharding import PartitionSpec as P

PANEL = 1024
HIGH = lax.Precision.HIGHEST
f32 = jnp.float32
bf16 = jnp.bfloat16
MIB = 2**20


def times_transposed(a, b, precision=HIGH):
    return lax.dot_general(
        a, b, (((1,), (1,)), ((), ())), precision=precision, preferred_element_type=f32
    )


def times(a, b):
    return lax.dot_general(
        a, b, (((1,), (0,)), ((), ())), precision=HIGH, preferred_element_type=f32
    )


def place_kernel(rows_ref, child_ref, out_ref):
    width = out_ref.shape[-1]
    position = lax.broadcasted_iota(jnp.int32, (128, 128), 0)
    for slot in range(4):
        hot = jnp.where(rows_ref[0, slot : slot + 1, :] == position, 1.0, 0.0).astype(bf16)
        placed = jnp.dot(hot, child_ref[slot], preferred_element_type=f32).astype(bf16)
        for jp in range(8):
            for jc in range(4):
                out_ref[jp, jc, slot] = placed[
                    jp * 16 : jp * 16 + 16, jc * width : jc * width + width
                ]


def place(rows, child_tiles, width, block):
    slots = child_tiles.shape[0]
    return pl.pallas_call(
        place_kernel,
        grid=(slots // 4,),
        in_specs=[
            pl.BlockSpec((1, 4, 128), lambda t: (t, 0, 0)),
            pl.BlockSpec((4, 128, 4 * width), lambda t: (t, 0, block)),
        ],
        out_specs=pl.BlockSpec((8, 4, 4, 16, width), lambda t: (0, 0, t, 0, 0)),
        out_shape=jax.ShapeDtypeStruct((8, 4, slots, 16, width), bf16),
        compiler_params=pltpu.CompilerParams(vmem_limit_bytes=56 * MIB),
        cost_estimate=pl.CostEstimate(
            flops=2 * slots * 128 * 128 * 4 * width,
            bytes_accessed=2 * slots * 128 * 4 * width * 2,
            transcendentals=0,
        ),
        name="place_rows",
    )(rows.reshape(slots // 4, 4, 128), child_tiles)


def collect_kernel(at_ref, got_ref, *refs):
    out_ref, odd_ref = refs[-2:]
    step = pl.program_id(0)

    @pl.when(step == 0)
    def _():
        out_ref[...] = jnp.zeros_like(out_ref)
        odd_ref[...] = jnp.zeros_like(odd_ref)

    sources, slots = got_ref.shape[:2]

    def add(pair, carry):
        source = pair * 2
        base = (step * sources + source) * slots
        for slot in range(slots):
            at, odd = at_ref[base + slot], at_ref[base + slots + slot]
            out_ref[at] = out_ref[at] + got_ref[source, slot].astype(f32)
            odd_ref[odd] = odd_ref[odd] + got_ref[source + 1, slot].astype(f32)
        return carry

    lax.fori_loop(0, sources // 2, add, 0)

    @pl.when(step == pl.num_programs(0) - 1)
    def _():
        out_ref[...] = out_ref[...] + odd_ref[...]


def collect(at, got, *after):
    sources, slots, _, width = got.shape
    return pl.pallas_call(
        collect_kernel,
        grid_spec=pltpu.PrefetchScalarGridSpec(
            num_scalar_prefetch=1,
            grid=(sources // 4,),
            in_specs=[pl.BlockSpec((4, slots, 16, width), lambda s, at: (s, 0, 0, 0))]
            + [pl.BlockSpec(memory_space=pl.ANY)] * len(after),
            out_specs=pl.BlockSpec((256, 16, width), lambda s, at: (0, 0, 0)),
            scratch_shapes=[pltpu.VMEM((256, 16, width), f32)],
        ),
        out_shape=jax.ShapeDtypeStruct((256, 16, width), f32),
        compiler_params=pltpu.CompilerParams(vmem_limit_bytes=56 * MIB),
        cost_estimate=pl.CostEstimate(
            flops=sources * slots * 16 * width,
            bytes_accessed=sources * slots * 16 * width * 2 + 256 * 16 * width * 4,
            transcendentals=0,
        ),
        name="collect_parents",
    )(at, got, *after)


def factor_block(block, u_ref, w_ref):
    sub = lax.broadcasted_iota(jnp.int32, (8, 128), 0)
    lane = lax.broadcasted_iota(jnp.int32, (8, 128), 1)

    def full(x):
        return jnp.broadcast_to(x, (8, 128))

    s = [block[8 * g : 8 * g + 8, :] for g in range(16)]
    v = [jnp.where(lane == sub + 8 * g, 1.0, 0.0).astype(f32) for g in range(16)]
    for b in range(16):
        cols = [full(s[b][:, 8 * b + j : 8 * b + j + 1]) for j in range(8)]
        e = [[full(cols[j][i : i + 1, :]) for j in range(i + 1)] for i in range(8)]
        inv, w, roots = [], [], []
        f = [[None] * 8 for _ in range(8)]
        for t in range(8):
            pivot = e[t][t]
            inv.append(1.0 / pivot)
            root = lax.rsqrt(pivot)
            roots.append(root * (1.5 - 0.5 * pivot * root * root))
            for i in range(t + 1, 8):
                f[i][t] = e[i][t] * inv[t]
            for i in range(t + 1, 8):
                for j in range(t + 1, i + 1):
                    e[i][j] = e[i][j] - f[i][t] * e[j][t]
        for i in range(8):
            r = []
            for j in range(i):
                acc = f[i][j]
                for k in range(j + 1, i):
                    acc = acc + f[i][k] * w[k][j]
                r.append(-acc)
            w.append(r)
        rows, vrows = s[b], v[b]
        new, vnew, scale = rows, vrows, roots[0]
        for i in range(1, 8):
            scale = jnp.where(sub == i, roots[i], scale)
        for j in range(7):
            c = jnp.zeros((8, 128), f32)
            for i in range(j + 1, 8):
                c = jnp.where(sub == i, w[i][j], c)
            new = new + c * full(rows[j : j + 1, :])
            vnew = vnew + c * full(vrows[j : j + 1, :])
        u_ref[8 * b : 8 * b + 8, :] = jnp.where(lane >= sub + 8 * b, new * scale, 0.0)
        w_ref[8 * b : 8 * b + 8, :] = vnew * scale
        if b == 15:
            break
        wi = [[w[t][j] * inv[t] for j in range(t)] for t in range(8)]
        brow = [full(new[t : t + 1, :]) for t in range(8)]
        bvrow = [full(vnew[t : t + 1, :]) for t in range(8)]
        for g in range(b + 1, 16):
            c = [full(s[g][:, 8 * b + j : 8 * b + j + 1]) for j in range(8)]
            for t in range(8):
                m = inv[t] * c[t]
                for j in range(t):
                    m = m + wi[t][j] * c[j]
                s[g] = s[g] - m * brow[t]
                v[g] = v[g] - m * bvrow[t]


def factor_kernel(index_ref, *refs):
    pieces, (l_ref, x_ref, a_ref, u_ref, w_ref) = refs[:8], refs[8:]
    for part, ref in enumerate(pieces):
        for n in range(4):
            j = index_ref[part * 4 + n]
            cols = pl.ds(pl.multiple_of(j % 4 * 256, 256), 256)
            for tile in range(8):
                rows = pl.ds(pl.multiple_of(tile * 128 + j // 4 * 16, 16), 16)
                a_ref[rows, cols] = ref[n, tile]
    l_ref[...] = jnp.zeros_like(l_ref)
    x_ref[...] = jnp.zeros_like(x_ref)
    for i in range(8):
        for j in range(i + 1):
            bi, bj = slice(128 * i, 128 * i + 128), slice(128 * j, 128 * j + 128)
            a_ref[bi, bj] = 0.5 * (a_ref[bi, bj] + a_ref[bj, bi].T)

    def step(b, carry):
        at = pl.ds(pl.multiple_of(b * 128, 128), 128)
        factor_block(a_ref[at, at], u_ref, w_ref)
        w = w_ref[...]
        l_ref[at, at] = u_ref[...].T
        x_ref[at, at] = w
        for n in range(8):

            @pl.when(b == n)
            def _():
                here = slice(128 * n, 128 * n + 128)
                if n < 7:
                    below = slice(128 * n + 128, PANEL)
                    low = times_transposed(a_ref[below, here], w)
                    l_ref[below, here] = low
                    for j in range(n + 1, 8):
                        rows, cols = slice(128 * j, PANEL), slice(128 * j, 128 * j + 128)
                        off = 128 * (j - n - 1)
                        a_ref[rows, cols] = a_ref[rows, cols] - times_transposed(
                            low[off:], low[off : off + 128]
                        )
                if n > 0:
                    done = slice(0, 128 * n)
                    x_ref[here, done] = -times(w, times(l_ref[here, done], x_ref[done, done]))

        return carry

    lax.fori_loop(0, 8, step, 0)


def factor(index, pieces):
    whole = pl.BlockSpec(memory_space=pltpu.VMEM)
    return pl.pallas_call(
        factor_kernel,
        in_specs=[pl.BlockSpec(memory_space=pltpu.SMEM)] + [whole] * 8,
        out_specs=[whole, whole],
        out_shape=[jax.ShapeDtypeStruct((PANEL, PANEL), f32)] * 2,
        scratch_shapes=[
            pltpu.VMEM((PANEL, PANEL), f32),
            pltpu.VMEM((128, 128), f32),
            pltpu.VMEM((128, 128), f32),
        ],
        compiler_params=pltpu.CompilerParams(vmem_limit_bytes=40 * MIB),
        cost_estimate=pl.CostEstimate(
            flops=7 * 10**10, bytes_accessed=12 * MIB, transcendentals=0
        ),
        name="factor_and_invert",
    )(index, *pieces)


def assemble_kernel(front_ref, got_ref, out_ref):
    for tile in range(2):
        for jc in range(4):
            cols = slice(jc * 256, jc * 256 + 256)
            sums = got_ref[:, jc, tile].reshape(128, 256)
            out_ref[tile, :, cols] = front_ref[tile, 0, :, cols] + sums


def assemble(front, got):
    k = front.shape[0]
    return pl.pallas_call(
        assemble_kernel,
        grid=(k // 2,),
        in_specs=[
            pl.BlockSpec((2, 1, 128, PANEL), lambda i: (i, 0, 0, 0)),
            pl.BlockSpec((8, 4, 2, 16, 256), lambda i: (0, 0, i, 0, 0)),
        ],
        out_specs=pl.BlockSpec((2, 128, PANEL), lambda i: (i, 0, 0)),
        out_shape=jax.ShapeDtypeStruct((k, 128, PANEL), f32),
        compiler_params=pltpu.CompilerParams(vmem_limit_bytes=56 * MIB),
        cost_estimate=pl.CostEstimate(
            flops=k * 128 * PANEL, bytes_accessed=12 * MIB, transcendentals=0
        ),
        name="assemble_panel",
    )(front, got)


def finish_kernel(order_ref, index_ref, panel_ref, lower_ref, top_ref, front_ref, got_ref, *refs):
    spread, pieces, (out_ref, slab_ref, rows_ref) = refs[:5], refs[5:13], refs[13:]
    step = pl.program_id(0)
    tiles = panel_ref.shape[0]
    leading = order_ref[4] == 0

    @pl.when(step == 0)
    def _():
        for part, ref in enumerate(pieces):
            for n in range(4):
                j = index_ref[part * 4 + n]
                for q in range(3):
                    at = (j % 4 * 3 + q) * 128 + j // 4 * 16
                    slab_ref[pl.ds(pl.multiple_of(at, 16), 16), :] = ref[n, q]

    for number in range(4):

        @pl.when(step == number)
        def _():
            if number == 2:
                rows_ref[:128, :] = spread[2][...]
                rows_ref[128:, :] = spread[3][...]
            else:
                rows_ref[...] = spread[number + number // 3][...]

    rows = rows_ref[...]

    @pl.when(leading)
    def _():
        out_ref[:, 0, :, :PANEL] = lower_ref[...]

    @pl.when(leading & (order_ref[step] == 0) & (order_ref[5] < 8))
    def _():
        out_ref[0, 0, :, :PANEL] = top_ref[...]

    @pl.when(jnp.logical_not(leading))
    def _():
        update = times_transposed(rows, slab_ref[:PANEL, :], None)
        out_ref[:, 0, :, :PANEL] = panel_ref[...] - update.reshape(tiles, 128, PANEL)

    update = times_transposed(rows, slab_ref[PANEL:, :], None).reshape(tiles, 128, -1)
    for jc in range(4):
        for tile in range(tiles):
            cols = slice(jc * 128, jc * 128 + 128)
            sums = got_ref[:, jc, tile].reshape(128, 128)
            out_ref[tile, 0, :, PANEL + jc * 128 : PANEL + jc * 128 + 128] = (
                front_ref[tile, 0, :, cols] + sums - update[tile, :, cols]
            )


def finish(order, index, panel, lower, top, front, got, spread, pieces):
    k, _, _, width = front.shape
    step = k // 4
    return pl.pallas_call(
        finish_kernel,
        grid_spec=pltpu.PrefetchScalarGridSpec(
            num_scalar_prefetch=2,
            grid=(4,),
            in_specs=[
                pl.BlockSpec((step, 128, PANEL), lambda i, o, _: (o[i], 0, 0)),
                pl.BlockSpec((step, 128, PANEL), lambda i, o, _: (o[i], 0, 0)),
                pl.BlockSpec((128, PANEL), lambda i, o, _: (0, 0)),
                pl.BlockSpec((step, 1, 128, 512), lambda i, o, _: (o[i], 0, 0, 2)),
                pl.BlockSpec((8, 4, step, 16, 128), lambda i, o, _: (0, 0, o[i], 0, 0)),
            ]
            + [pl.BlockSpec(x.shape, lambda i, o, _: (0, 0)) for x in spread]
            + [pl.BlockSpec(x.shape, lambda i, o, _: (0, 0, 0, 0)) for x in pieces],
            out_specs=pl.BlockSpec((step, 1, 128, width), lambda i, o, _: (o[i], 0, 0, 0)),
            scratch_shapes=[
                pltpu.VMEM((width, PANEL), bf16),
                pltpu.VMEM((step * 128, PANEL), bf16),
            ],
        ),
        out_shape=jax.ShapeDtypeStruct(front.shape, f32),
        compiler_params=pltpu.CompilerParams(vmem_limit_bytes=60 * MIB),
        cost_estimate=pl.CostEstimate(
            flops=2 * k * 128 * width * PANEL,
            bytes_accessed=28 * MIB,
            transcendentals=0,
        ),
        name="trailing_update",
    )(order, index, panel, lower, top, front, got, *spread, *pieces)


def exchange(x):
    return lax.all_to_all(x, "row", split_axis=0, concat_axis=0, tiled=True)


def row_number(x, z, core):
    return (x % 4 * 4 + z % 4) * 2 + core


def ring_stage(x, stage):
    parts = [x]
    for by in range(1, 4):
        moves = []
        for chip in range(16):
            for core in range(2):
                along_z = core == stage
                to = row_number(
                    chip // 4 + (0 if along_z else by), chip % 4 + (by if along_z else 0), core
                )
                moves.append((chip * 2 + core, to))
        parts.append(lax.ppermute(x, "row", moves))
    return parts


def with_cores(mine):
    return mine + [lax.ppermute(part, "row", [(r, r ^ 1) for r in range(32)]) for part in mine]


def gathered_index(row_index):
    number = jnp.arange(32, dtype=jnp.int32)
    half, outer, inner = number // 16, number // 4 % 4, number % 4
    core = (row_index + half) % 2
    chip = row_index // 2
    x = chip // 4 - jnp.where(core == 0, outer, inner) + 4
    z = chip % 4 - jnp.where(core == 0, inner, outer) + 4
    return row_number(x, z, core)


def exchange_by_permutes(x, row_index):
    rest = x.shape[1:]
    core, z, along = row_index % 2, row_index // 2 % 4, row_index // 8
    x = x.reshape((4, 4, 2) + rest)
    keep = jnp.where(core == 0, x[:, :, 0], x[:, :, 1])
    send = jnp.where(core == 0, x[:, :, 1], x[:, :, 0])
    x = jnp.stack([keep, lax.ppermute(send, "row", [(r, r ^ 1) for r in range(32)])])
    for stage, place_now in enumerate((z, along)):
        parts = []
        for by in range(4):
            part = lax.dynamic_index_in_dim(x, (place_now + by) % 4, x.ndim - len(rest) - 1, False)
            if by:
                moves = []
                for r in range(32):
                    there = (r // 8, r // 2 % 4 + by) if stage == 0 else (r // 8 + by, r // 2 % 4)
                    moves.append((r, row_number(*there, r % 2)))
                part = lax.ppermute(part, "row", moves)
            parts.append(part)
        x = jnp.stack(parts)
    source = jnp.arange(32, dtype=jnp.int32)
    at = (along - source // 8 + 4) % 4 * 8 + (z - source // 2 % 4 + 4) % 4 * 2
    at = at + (core ^ (source % 2))
    return jnp.take(x.reshape((32,) + rest), at, axis=0, mode="clip")


def from_first(pieces, col_index):
    result = jnp.where(col_index == 0, pieces[0], 0)
    for c in range(1, len(pieces)):
        result = result + lax.ppermute(pieces[c], "col", [(0, c)])
    return result


def own_rows(tiles, row_index):
    tiles = tiles.reshape(4, 3, 16, 256)
    quarter = row_index % 4
    result = jnp.zeros((3, 16, PANEL), f32)
    for by in range(4):
        part = lax.dynamic_index_in_dim(tiles, quarter ^ by, 0, keepdims=False)
        if by:
            part = lax.ppermute(part, "row", [(r, r ^ by) for r in range(32)])
        result = lax.dynamic_update_slice(result, part, (0, 0, (quarter ^ by) * 256))
    return result.reshape(48, PANEL)


def together(*arrays):
    return lax.optimization_barrier(arrays)


def body(front, child_tiles, tile_parent, tile_rows, tile_count):
    row_index = lax.axis_index("row").astype(jnp.int32)
    col_index = lax.axis_index("col").astype(jnp.int32)
    slots = child_tiles.shape[0]
    index = gathered_index(row_index)
    live = jnp.arange(slots, dtype=jnp.int32) < tile_count[0]
    rows = jnp.where(live[:, None], tile_rows, -1)
    at = (tile_parent % 32) * 8 + tile_parent // 32

    early = front[:2, 0, :, :PANEL].reshape(2, 8, 16, 4, 256).transpose(1, 3, 0, 2, 4)
    at = jnp.pad(at.astype(f32).reshape(1, slots), ((0, 7), (0, 256 - slots)))
    early = jnp.concatenate(
        [early.reshape(32, 32, 256), jnp.broadcast_to(at[None], (32, 8, 256))], axis=1
    )
    early = exchange_by_permutes(early, row_index)
    at = early[:, 32, :slots].astype(jnp.int32).reshape(32 * slots)
    early = early[:, :32].reshape(32, 2, 16, 256)

    sent = place(rows, child_tiles, 256, 0).reshape(32, slots, 16, 256)
    sent_rest = place(rows, child_tiles, 128, 2).reshape(32, slots, 16, 128)
    got, sent_rest = together(exchange(sent), sent_rest)
    sums = collect(at, got).reshape(32, 8, 16, 256)

    tiles = (sums[:, :2] + early).transpose(1, 0, 2, 3).reshape(64, 16, 256)
    pieces = [jnp.concatenate([tiles[:8], tiles[12 * c : 12 * c + 12]]) for c in range(4)]
    piece = from_first(pieces, col_index)
    ring, part = together(jnp.stack(ring_stage(piece[:8], 0)), own_rows(piece[8:], row_index))
    diagonal = with_cores(ring_stage(ring, 1))

    got, sent_rest = together(exchange(sums), sent_rest)
    panel = assemble(front, got.reshape(8, 4, 8, 16, 256))
    own = from_first([panel[2 * c : 2 * c + 2] for c in range(4)], col_index)
    got_rest = exchange(sent_rest)

    factored, inverse = factor(index, diagonal)

    def rows_of_factor(start, count):
        start = jnp.minimum(start, PANEL - count)
        return lax.dynamic_slice_in_dim(factored, start, count, 0)

    top = rows_of_factor(row_index * 128, 128)
    known, tile = [top], 12 * col_index + 3 * (row_index % 4)
    for q in range(3):
        known.append(rows_of_factor((tile + q) * 128 + row_index // 4 * 16, 16))
    known = jnp.concatenate(known)
    inside = jnp.concatenate(
        [
            jnp.broadcast_to((row_index < 8) & (col_index == 0), (128,)),
            jnp.repeat(tile + jnp.arange(3, dtype=jnp.int32) < 8, 16, total_repeat_length=48),
        ]
    )
    solved = jnp.concatenate([own.reshape(256, PANEL), part])
    solved = times_transposed(solved, inverse)
    both = jnp.concatenate([solved[:128], solved[256:]])
    both = jnp.where(inside[:, None], known, both).astype(bf16)
    own = jnp.concatenate([both[:128], solved[128:256].astype(bf16)])
    part = both[128:].reshape(3, 16, PANEL)

    def turn(x, by):
        return lax.ppermute(x, "col", [(c, (c + by) % 4) for c in range(4)])

    before, behind = turn(own, 1), turn(own, 3)
    sums_rest = collect(at, got_rest, own, part)
    ring, sums_rest, before, behind = together(
        jnp.stack(ring_stage(part, 0)), sums_rest, before, behind
    )
    got_rest = exchange(sums_rest.reshape(32, 8, 16, 128)).reshape(8, 4, 8, 16, 128)
    lower = times_transposed(panel.reshape(8 * 128, PANEL), inverse).reshape(8, 128, PANEL)
    far = turn(before[:128], 1), turn(behind[128:], 3)
    *mine, lower, far_before, far_behind = together(*ring_stage(ring, 1), lower, *far)
    spread = [own, before, far_before, far_behind, behind]
    slab = with_cores(mine)

    order = (col_index + 4 - jnp.arange(4, dtype=jnp.int32)) % 4
    order = jnp.concatenate([order, jnp.stack([col_index, row_index])])
    return finish(order, index, panel, lower, top, front, got_rest, spread, slab)


def solution(mesh):
    placed = (
        P(None, "row", None, "col"),
        P("row", None, "col"),
        P("row"),
        P("row", None),
        P("row"),
    )
    return jax.shard_map(
        body, mesh=mesh, in_specs=placed, out_specs=P(None, "row", None, "col"), check_vma=False
    )
```

```python
import jax
import jax.numpy as jnp
from jax import lax
from jax.experimental import pallas as pl
from jax.experimental.pallas import tpu as pltpu
from jax.sharding import PartitionSpec as P

PANEL = 1024
HIGH = lax.Precision.HIGHEST
f32 = jnp.float32
bf16 = jnp.bfloat16
MIB = 2**20


def times_transposed(a, b, precision=HIGH):
    return lax.dot_general(
        a, b, (((1,), (1,)), ((), ())), precision=precision, preferred_element_type=f32
    )


def times(a, b):
    return lax.dot_general(
        a, b, (((1,), (0,)), ((), ())), precision=HIGH, preferred_element_type=f32
    )


def place_kernel(rows_ref, child_ref, out_ref):
    width = out_ref.shape[-1]
    position = lax.broadcasted_iota(jnp.int32, (128, 128), 0)
    for slot in range(4):
        hot = jnp.where(rows_ref[0, slot : slot + 1, :] == position, 1.0, 0.0).astype(bf16)
        placed = jnp.dot(hot, child_ref[slot], preferred_element_type=f32).astype(bf16)
        for jp in range(8):
            for jc in range(4):
                out_ref[jp, jc, slot] = placed[
                    jp * 16 : jp * 16 + 16, jc * width : jc * width + width
                ]


def place(rows, child_tiles, width, block):
    slots = child_tiles.shape[0]
    return pl.pallas_call(
        place_kernel,
        grid=(slots // 4,),
        in_specs=[
            pl.BlockSpec((1, 4, 128), lambda t: (t, 0, 0)),
            pl.BlockSpec((4, 128, 4 * width), lambda t: (t, 0, block)),
        ],
        out_specs=pl.BlockSpec((8, 4, 4, 16, width), lambda t: (0, 0, t, 0, 0)),
        out_shape=jax.ShapeDtypeStruct((8, 4, slots, 16, width), bf16),
        compiler_params=pltpu.CompilerParams(vmem_limit_bytes=56 * MIB),
        cost_estimate=pl.CostEstimate(
            flops=2 * slots * 128 * 128 * 4 * width,
            bytes_accessed=2 * slots * 128 * 4 * width * 2,
            transcendentals=0,
        ),
        name="place_rows",
    )(rows.reshape(slots // 4, 4, 128), child_tiles)


def collect_kernel(at_ref, got_ref, *refs):
    out_ref, odd_ref = refs[-2:]
    step = pl.program_id(0)

    @pl.when(step == 0)
    def _():
        out_ref[...] = jnp.zeros_like(out_ref)
        odd_ref[...] = jnp.zeros_like(odd_ref)

    sources, slots = got_ref.shape[:2]

    def add(pair, carry):
        source = pair * 2
        base = (step * sources + source) * slots
        for slot in range(slots):
            at, odd = at_ref[base + slot], at_ref[base + slots + slot]
            out_ref[at] = out_ref[at] + got_ref[source, slot].astype(f32)
            odd_ref[odd] = odd_ref[odd] + got_ref[source + 1, slot].astype(f32)
        return carry

    lax.fori_loop(0, sources // 2, add, 0)

    @pl.when(step == pl.num_programs(0) - 1)
    def _():
        out_ref[...] = out_ref[...] + odd_ref[...]


def collect(at, got, *after):
    sources, slots, _, width = got.shape
    return pl.pallas_call(
        collect_kernel,
        grid_spec=pltpu.PrefetchScalarGridSpec(
            num_scalar_prefetch=1,
            grid=(sources // 4,),
            in_specs=[pl.BlockSpec((4, slots, 16, width), lambda s, at: (s, 0, 0, 0))]
            + [pl.BlockSpec(memory_space=pl.ANY)] * len(after),
            out_specs=pl.BlockSpec((256, 16, width), lambda s, at: (0, 0, 0)),
            scratch_shapes=[pltpu.VMEM((256, 16, width), f32)],
        ),
        out_shape=jax.ShapeDtypeStruct((256, 16, width), f32),
        compiler_params=pltpu.CompilerParams(vmem_limit_bytes=56 * MIB),
        cost_estimate=pl.CostEstimate(
            flops=sources * slots * 16 * width,
            bytes_accessed=sources * slots * 16 * width * 2 + 256 * 16 * width * 4,
            transcendentals=0,
        ),
        name="collect_parents",
    )(at, got, *after)


def factor_block(block, u_ref, w_ref):
    sub = lax.broadcasted_iota(jnp.int32, (8, 128), 0)
    lane = lax.broadcasted_iota(jnp.int32, (8, 128), 1)

    def full(x):
        return jnp.broadcast_to(x, (8, 128))

    s = [block[8 * g : 8 * g + 8, :] for g in range(16)]
    v = [jnp.where(lane == sub + 8 * g, 1.0, 0.0).astype(f32) for g in range(16)]
    for b in range(16):
        cols = [full(s[b][:, 8 * b + j : 8 * b + j + 1]) for j in range(8)]
        e = [[full(cols[j][i : i + 1, :]) for j in range(i + 1)] for i in range(8)]
        inv, w, roots = [], [], []
        f = [[None] * 8 for _ in range(8)]
        for t in range(8):
            pivot = e[t][t]
            inv.append(1.0 / pivot)
            root = lax.rsqrt(pivot)
            roots.append(root * (1.5 - 0.5 * pivot * root * root))
            for i in range(t + 1, 8):
                f[i][t] = e[i][t] * inv[t]
            for i in range(t + 1, 8):
                for j in range(t + 1, i + 1):
                    e[i][j] = e[i][j] - f[i][t] * e[j][t]
        for i in range(8):
            r = []
            for j in range(i):
                acc = f[i][j]
                for k in range(j + 1, i):
                    acc = acc + f[i][k] * w[k][j]
                r.append(-acc)
            w.append(r)
        rows, vrows = s[b], v[b]
        new, vnew, scale = rows, vrows, roots[0]
        for i in range(1, 8):
            scale = jnp.where(sub == i, roots[i], scale)
        for j in range(7):
            c = jnp.zeros((8, 128), f32)
            for i in range(j + 1, 8):
                c = jnp.where(sub == i, w[i][j], c)
            new = new + c * full(rows[j : j + 1, :])
            vnew = vnew + c * full(vrows[j : j + 1, :])
        u_ref[8 * b : 8 * b + 8, :] = jnp.where(lane >= sub + 8 * b, new * scale, 0.0)
        w_ref[8 * b : 8 * b + 8, :] = vnew * scale
        if b == 15:
            break
        wi = [[w[t][j] * inv[t] for j in range(t)] for t in range(8)]
        brow = [full(new[t : t + 1, :]) for t in range(8)]
        bvrow = [full(vnew[t : t + 1, :]) for t in range(8)]
        for g in range(b + 1, 16):
            c = [full(s[g][:, 8 * b + j : 8 * b + j + 1]) for j in range(8)]
            for t in range(8):
                m = inv[t] * c[t]
                for j in range(t):
                    m = m + wi[t][j] * c[j]
                s[g] = s[g] - m * brow[t]
                v[g] = v[g] - m * bvrow[t]


def factor_kernel(index_ref, *refs):
    pieces, (l_ref, x_ref, a_ref, u_ref, w_ref) = refs[:8], refs[8:]
    for part, ref in enumerate(pieces):
        for n in range(4):
            j = index_ref[part * 4 + n]
            cols = pl.ds(pl.multiple_of(j % 4 * 256, 256), 256)
            for tile in range(8):
                rows = pl.ds(pl.multiple_of(tile * 128 + j // 4 * 16, 16), 16)
                a_ref[rows, cols] = ref[n, tile]
    l_ref[...] = jnp.zeros_like(l_ref)
    x_ref[...] = jnp.zeros_like(x_ref)
    for i in range(8):
        for j in range(i + 1):
            bi, bj = slice(128 * i, 128 * i + 128), slice(128 * j, 128 * j + 128)
            a_ref[bi, bj] = 0.5 * (a_ref[bi, bj] + a_ref[bj, bi].T)

    def step(b, carry):
        at = pl.ds(pl.multiple_of(b * 128, 128), 128)
        factor_block(a_ref[at, at], u_ref, w_ref)
        w = w_ref[...]
        l_ref[at, at] = u_ref[...].T
        x_ref[at, at] = w
        for n in range(8):

            @pl.when(b == n)
            def _():
                here = slice(128 * n, 128 * n + 128)
                if n < 7:
                    below = slice(128 * n + 128, PANEL)
                    low = times_transposed(a_ref[below, here], w)
                    l_ref[below, here] = low
                    for j in range(n + 1, 8):
                        rows, cols = slice(128 * j, PANEL), slice(128 * j, 128 * j + 128)
                        off = 128 * (j - n - 1)
                        a_ref[rows, cols] = a_ref[rows, cols] - times_transposed(
                            low[off:], low[off : off + 128]
                        )
                if n > 0:
                    done = slice(0, 128 * n)
                    x_ref[here, done] = -times(w, times(l_ref[here, done], x_ref[done, done]))

        return carry

    lax.fori_loop(0, 8, step, 0)


def factor(index, pieces):
    whole = pl.BlockSpec(memory_space=pltpu.VMEM)
    return pl.pallas_call(
        factor_kernel,
        in_specs=[pl.BlockSpec(memory_space=pltpu.SMEM)] + [whole] * 8,
        out_specs=[whole, whole],
        out_shape=[jax.ShapeDtypeStruct((PANEL, PANEL), f32)] * 2,
        scratch_shapes=[
            pltpu.VMEM((PANEL, PANEL), f32),
            pltpu.VMEM((128, 128), f32),
            pltpu.VMEM((128, 128), f32),
        ],
        compiler_params=pltpu.CompilerParams(vmem_limit_bytes=40 * MIB),
        cost_estimate=pl.CostEstimate(
            flops=7 * 10**10, bytes_accessed=12 * MIB, transcendentals=0
        ),
        name="factor_and_invert",
    )(index, *pieces)


def assemble_kernel(front_ref, got_ref, out_ref):
    for tile in range(2):
        for jc in range(4):
            cols = slice(jc * 256, jc * 256 + 256)
            sums = got_ref[:, jc, tile].reshape(128, 256)
            out_ref[tile, :, cols] = front_ref[tile, 0, :, cols] + sums


def assemble(front, got):
    k = front.shape[0]
    return pl.pallas_call(
        assemble_kernel,
        grid=(k // 2,),
        in_specs=[
            pl.BlockSpec((2, 1, 128, PANEL), lambda i: (i, 0, 0, 0)),
            pl.BlockSpec((8, 4, 2, 16, 256), lambda i: (0, 0, i, 0, 0)),
        ],
        out_specs=pl.BlockSpec((2, 128, PANEL), lambda i: (i, 0, 0)),
        out_shape=jax.ShapeDtypeStruct((k, 128, PANEL), f32),
        compiler_params=pltpu.CompilerParams(vmem_limit_bytes=56 * MIB),
        cost_estimate=pl.CostEstimate(
            flops=k * 128 * PANEL, bytes_accessed=12 * MIB, transcendentals=0
        ),
        name="assemble_panel",
    )(front, got)


def finish_kernel(order_ref, index_ref, panel_ref, lower_ref, top_ref, front_ref, got_ref, *refs):
    spread, pieces, (out_ref, slab_ref, rows_ref) = refs[:5], refs[5:13], refs[13:]
    step = pl.program_id(0)
    tiles = panel_ref.shape[0]
    leading = order_ref[4] == 0

    @pl.when(step == 0)
    def _():
        for part, ref in enumerate(pieces):
            for n in range(4):
                j = index_ref[part * 4 + n]
                for q in range(3):
                    at = (j % 4 * 3 + q) * 128 + j // 4 * 16
                    slab_ref[pl.ds(pl.multiple_of(at, 16), 16), :] = ref[n, q]

    for number in range(4):

        @pl.when(step == number)
        def _():
            if number == 2:
                rows_ref[:128, :] = spread[2][...]
                rows_ref[128:, :] = spread[3][...]
            else:
                rows_ref[...] = spread[number + number // 3][...]

    rows = rows_ref[...]

    @pl.when(leading)
    def _():
        out_ref[:, 0, :, :PANEL] = lower_ref[...]

    @pl.when(leading & (order_ref[step] == 0) & (order_ref[5] < 8))
    def _():
        out_ref[0, 0, :, :PANEL] = top_ref[...]

    @pl.when(jnp.logical_not(leading))
    def _():
        update = times_transposed(rows, slab_ref[:PANEL, :], None)
        out_ref[:, 0, :, :PANEL] = panel_ref[...] - update.reshape(tiles, 128, PANEL)

    update = times_transposed(rows, slab_ref[PANEL:, :], None).reshape(tiles, 128, -1)
    for jc in range(4):
        for tile in range(tiles):
            cols = slice(jc * 128, jc * 128 + 128)
            sums = got_ref[:, jc, tile].reshape(128, 128)
            out_ref[tile, 0, :, PANEL + jc * 128 : PANEL + jc * 128 + 128] = (
                front_ref[tile, 0, :, cols] + sums - update[tile, :, cols]
            )


def finish(order, index, panel, lower, top, front, got, spread, pieces):
    k, _, _, width = front.shape
    step = k // 4
    return pl.pallas_call(
        finish_kernel,
        grid_spec=pltpu.PrefetchScalarGridSpec(
            num_scalar_prefetch=2,
            grid=(4,),
            in_specs=[
                pl.BlockSpec((step, 128, PANEL), lambda i, o, _: (o[i], 0, 0)),
                pl.BlockSpec((step, 128, PANEL), lambda i, o, _: (o[i], 0, 0)),
                pl.BlockSpec((128, PANEL), lambda i, o, _: (0, 0)),
                pl.BlockSpec((step, 1, 128, 512), lambda i, o, _: (o[i], 0, 0, 2)),
                pl.BlockSpec((8, 4, step, 16, 128), lambda i, o, _: (0, 0, o[i], 0, 0)),
            ]
            + [pl.BlockSpec(x.shape, lambda i, o, _: (0, 0)) for x in spread]
            + [pl.BlockSpec(x.shape, lambda i, o, _: (0, 0, 0, 0)) for x in pieces],
            out_specs=pl.BlockSpec((step, 1, 128, width), lambda i, o, _: (o[i], 0, 0, 0)),
            scratch_shapes=[
                pltpu.VMEM((width, PANEL), bf16),
                pltpu.VMEM((step * 128, PANEL), bf16),
            ],
        ),
        out_shape=jax.ShapeDtypeStruct(front.shape, f32),
        compiler_params=pltpu.CompilerParams(vmem_limit_bytes=60 * MIB),
        cost_estimate=pl.CostEstimate(
            flops=2 * k * 128 * width * PANEL,
            bytes_accessed=28 * MIB,
            transcendentals=0,
        ),
        name="trailing_update",
    )(order, index, panel, lower, top, front, got, *spread, *pieces)


def exchange(x):
    return lax.all_to_all(x, "row", split_axis=0, concat_axis=0, tiled=True)


def row_number(x, z, core):
    return (x % 4 * 4 + z % 4) * 2 + core


def ring_stage(x, stage):
    parts = [x]
    for by in range(1, 4):
        moves = []
        for chip in range(16):
            for core in range(2):
                along_z = core == stage
                to = row_number(
                    chip // 4 + (0 if along_z else by), chip % 4 + (by if along_z else 0), core
                )
                moves.append((chip * 2 + core, to))
        parts.append(lax.ppermute(x, "row", moves))
    return parts


def with_cores(mine):
    return mine + [lax.ppermute(part, "row", [(r, r ^ 1) for r in range(32)]) for part in mine]


def gathered_index(row_index):
    number = jnp.arange(32, dtype=jnp.int32)
    half, outer, inner = number // 16, number // 4 % 4, number % 4
    core = (row_index + half) % 2
    chip = row_index // 2
    x = chip // 4 - jnp.where(core == 0, outer, inner) + 4
    z = chip % 4 - jnp.where(core == 0, inner, outer) + 4
    return row_number(x, z, core)


def exchange_by_permutes(x, row_index, other):
    rest = x.shape[1:]
    core, z, along = row_index % 2, row_index // 2 % 4, row_index // 8
    x = x.reshape((4, 4, 2) + rest)
    keep = jnp.where(core == 0, x[:, :, 0], x[:, :, 1])
    send = jnp.where(core == 0, x[:, :, 1], x[:, :, 0])
    x = jnp.stack([keep, lax.ppermute(send, "row", [(r, r ^ 1) for r in range(32)])])
    for stage, place_now in enumerate((z, along)):
        parts = []
        for by in range(4):
            part = lax.dynamic_index_in_dim(x, (place_now + by) % 4, x.ndim - len(rest) - 1, False)
            if by:
                moves = []
                for r in range(32):
                    there = (r // 8, r // 2 % 4 + by) if stage == 0 else (r // 8 + by, r // 2 % 4)
                    moves.append((r, row_number(*there, r % 2)))
                part = lax.ppermute(part, "row", moves)
            parts.append(part)
        x = jnp.stack(parts)
        if stage == 0:
            x, other = together(x, other)
    source = jnp.arange(32, dtype=jnp.int32)
    at = (along - source // 8 + 4) % 4 * 8 + (z - source // 2 % 4 + 4) % 4 * 2
    at = at + (core ^ (source % 2))
    return jnp.take(x.reshape((32,) + rest), at, axis=0, mode="clip"), other


def from_first(pieces, col_index):
    result = jnp.where(col_index == 0, pieces[0], 0)
    for c in range(1, len(pieces)):
        result = result + lax.ppermute(pieces[c], "col", [(0, c)])
    return result


def own_rows(tiles, row_index):
    tiles = tiles.reshape(4, 3, 16, 256)
    quarter = row_index % 4
    result = jnp.zeros((3, 16, PANEL), f32)
    for by in range(4):
        part = lax.dynamic_index_in_dim(tiles, quarter ^ by, 0, keepdims=False)
        if by:
            part = lax.ppermute(part, "row", [(r, r ^ by) for r in range(32)])
        result = lax.dynamic_update_slice(result, part, (0, 0, (quarter ^ by) * 256))
    return result.reshape(48, PANEL)


def together(*arrays):
    return lax.optimization_barrier(arrays)


def body(front, child_tiles, tile_parent, tile_rows, tile_count):
    row_index = lax.axis_index("row").astype(jnp.int32)
    col_index = lax.axis_index("col").astype(jnp.int32)
    slots = child_tiles.shape[0]
    index = gathered_index(row_index)
    live = jnp.arange(slots, dtype=jnp.int32) < tile_count[0]
    rows = jnp.where(live[:, None], tile_rows, -1)
    at = (tile_parent % 32) * 8 + tile_parent // 32

    early = front[:2, 0, :, :PANEL].reshape(2, 8, 16, 4, 256).transpose(1, 3, 0, 2, 4)
    at = jnp.pad(at.astype(f32).reshape(1, slots), ((0, 7), (0, 256 - slots)))
    early = jnp.concatenate(
        [early.reshape(32, 32, 256), jnp.broadcast_to(at[None], (32, 8, 256))], axis=1
    )
    sent_rest = place(rows, child_tiles, 128, 2).reshape(32, slots, 16, 128)
    early, sent_rest = exchange_by_permutes(early, row_index, sent_rest)
    at = early[:, 32, :slots].astype(jnp.int32).reshape(32 * slots)
    early = early[:, :32].reshape(32, 2, 16, 256)

    sent = place(rows, child_tiles, 256, 0).reshape(32, slots, 16, 256)
    got, sent_rest = together(exchange(sent), sent_rest)
    sums = collect(at, got).reshape(32, 8, 16, 256)

    tiles = (sums[:, :2] + early).transpose(1, 0, 2, 3).reshape(64, 16, 256)
    pieces = [jnp.concatenate([tiles[:8], tiles[12 * c : 12 * c + 12]]) for c in range(4)]
    piece = from_first(pieces, col_index)
    ring, part = together(jnp.stack(ring_stage(piece[:8], 0)), own_rows(piece[8:], row_index))
    diagonal = with_cores(ring_stage(ring, 1))

    got, sent_rest = together(exchange(sums), sent_rest)
    panel = assemble(front, got.reshape(8, 4, 8, 16, 256))
    own = from_first([panel[2 * c : 2 * c + 2] for c in range(4)], col_index)
    got_rest = exchange(sent_rest)

    factored, inverse = factor(index, diagonal)

    def rows_of_factor(start, count):
        start = jnp.minimum(start, PANEL - count)
        return lax.dynamic_slice_in_dim(factored, start, count, 0)

    top = rows_of_factor(row_index * 128, 128)
    known, tile = [top], 12 * col_index + 3 * (row_index % 4)
    for q in range(3):
        known.append(rows_of_factor((tile + q) * 128 + row_index // 4 * 16, 16))
    known = jnp.concatenate(known)
    inside = jnp.concatenate(
        [
            jnp.broadcast_to((row_index < 8) & (col_index == 0), (128,)),
            jnp.repeat(tile + jnp.arange(3, dtype=jnp.int32) < 8, 16, total_repeat_length=48),
        ]
    )
    solved = jnp.concatenate([own.reshape(256, PANEL), part])
    solved = times_transposed(solved, inverse)
    both = jnp.concatenate([solved[:128], solved[256:]])
    both = jnp.where(inside[:, None], known, both).astype(bf16)
    own = jnp.concatenate([both[:128], solved[128:256].astype(bf16)])
    part = both[128:].reshape(3, 16, PANEL)

    def turn(x, by):
        return lax.ppermute(x, "col", [(c, (c + by) % 4) for c in range(4)])

    before, behind = turn(own, 1), turn(own, 3)
    sums_rest = collect(at, got_rest, own, part)
    ring, sums_rest, before, behind = together(
        jnp.stack(ring_stage(part, 0)), sums_rest, before, behind
    )
    got_rest = exchange(sums_rest.reshape(32, 8, 16, 128)).reshape(8, 4, 8, 16, 128)
    lower = times_transposed(panel.reshape(8 * 128, PANEL), inverse).reshape(8, 128, PANEL)
    far = turn(before[:128], 1), turn(behind[128:], 3)
    *mine, lower, far_before, far_behind = together(*ring_stage(ring, 1), lower, *far)
    spread = [own, before, far_before, far_behind, behind]
    slab = with_cores(mine)

    order = (col_index + 4 - jnp.arange(4, dtype=jnp.int32)) % 4
    order = jnp.concatenate([order, jnp.stack([col_index, row_index])])
    return finish(order, index, panel, lower, top, front, got_rest, spread, slab)


def solution(mesh):
    placed = (
        P(None, "row", None, "col"),
        P("row", None, "col"),
        P("row"),
        P("row", None),
        P("row"),
    )
    return jax.shard_map(
        body, mesh=mesh, in_specs=placed, out_specs=P(None, "row", None, "col"), check_vma=False
    )
```

```python
import jax
import jax.numpy as jnp
from jax import lax
from jax.experimental import pallas as pl
from jax.experimental.pallas import tpu as pltpu
from jax.sharding import PartitionSpec as P

PANEL = 1024
HIGH = lax.Precision.HIGHEST
f32 = jnp.float32
bf16 = jnp.bfloat16
MIB = 2**20


def times_transposed(a, b, precision=HIGH):
    return lax.dot_general(
        a, b, (((1,), (1,)), ((), ())), precision=precision, preferred_element_type=f32
    )


def times(a, b):
    return lax.dot_general(
        a, b, (((1,), (0,)), ((), ())), precision=HIGH, preferred_element_type=f32
    )


def place_kernel(rows_ref, child_ref, out_ref):
    width = out_ref.shape[-1]
    position = lax.broadcasted_iota(jnp.int32, (128, 128), 0)
    for slot in range(4):
        hot = jnp.where(rows_ref[0, slot : slot + 1, :] == position, 1.0, 0.0).astype(bf16)
        placed = jnp.dot(hot, child_ref[slot], preferred_element_type=f32).astype(bf16)
        for jp in range(8):
            for jc in range(4):
                out_ref[jp, jc, slot] = placed[
                    jp * 16 : jp * 16 + 16, jc * width : jc * width + width
                ]


def place(rows, child_tiles, width, block):
    slots = child_tiles.shape[0]
    return pl.pallas_call(
        place_kernel,
        grid=(slots // 4,),
        in_specs=[
            pl.BlockSpec((1, 4, 128), lambda t: (t, 0, 0)),
            pl.BlockSpec((4, 128, 4 * width), lambda t: (t, 0, block)),
        ],
        out_specs=pl.BlockSpec((8, 4, 4, 16, width), lambda t: (0, 0, t, 0, 0)),
        out_shape=jax.ShapeDtypeStruct((8, 4, slots, 16, width), bf16),
        compiler_params=pltpu.CompilerParams(vmem_limit_bytes=56 * MIB),
        cost_estimate=pl.CostEstimate(
            flops=2 * slots * 128 * 128 * 4 * width,
            bytes_accessed=2 * slots * 128 * 4 * width * 2,
            transcendentals=0,
        ),
        name="place_rows",
    )(rows.reshape(slots // 4, 4, 128), child_tiles)


def collect_kernel(at_ref, got_ref, *refs):
    out_ref, odd_ref = refs[-2:]
    step = pl.program_id(0)

    @pl.when(step == 0)
    def _():
        out_ref[...] = jnp.zeros_like(out_ref)
        odd_ref[...] = jnp.zeros_like(odd_ref)

    sources, slots = got_ref.shape[:2]

    def add(pair, carry):
        source = pair * 2
        base = (step * sources + source) * slots
        for slot in range(slots):
            at, odd = at_ref[base + slot], at_ref[base + slots + slot]
            out_ref[at] = out_ref[at] + got_ref[source, slot].astype(f32)
            odd_ref[odd] = odd_ref[odd] + got_ref[source + 1, slot].astype(f32)
        return carry

    lax.fori_loop(0, sources // 2, add, 0)

    @pl.when(step == pl.num_programs(0) - 1)
    def _():
        out_ref[...] = out_ref[...] + odd_ref[...]


def collect(at, got, *after):
    sources, slots, _, width = got.shape
    return pl.pallas_call(
        collect_kernel,
        grid_spec=pltpu.PrefetchScalarGridSpec(
            num_scalar_prefetch=1,
            grid=(sources // 4,),
            in_specs=[pl.BlockSpec((4, slots, 16, width), lambda s, at: (s, 0, 0, 0))]
            + [pl.BlockSpec(memory_space=pl.ANY)] * len(after),
            out_specs=pl.BlockSpec((256, 16, width), lambda s, at: (0, 0, 0)),
            scratch_shapes=[pltpu.VMEM((256, 16, width), f32)],
        ),
        out_shape=jax.ShapeDtypeStruct((256, 16, width), f32),
        compiler_params=pltpu.CompilerParams(vmem_limit_bytes=56 * MIB),
        cost_estimate=pl.CostEstimate(
            flops=sources * slots * 16 * width,
            bytes_accessed=sources * slots * 16 * width * 2 + 256 * 16 * width * 4,
            transcendentals=0,
        ),
        name="collect_parents",
    )(at, got, *after)


def factor_block(block, u_ref, w_ref):
    sub = lax.broadcasted_iota(jnp.int32, (8, 128), 0)
    lane = lax.broadcasted_iota(jnp.int32, (8, 128), 1)

    def full(x):
        return jnp.broadcast_to(x, (8, 128))

    s = [block[8 * g : 8 * g + 8, :] for g in range(16)]
    v = [jnp.where(lane == sub + 8 * g, 1.0, 0.0).astype(f32) for g in range(16)]
    for b in range(16):
        cols = [full(s[b][:, 8 * b + j : 8 * b + j + 1]) for j in range(8)]
        e = [[full(cols[j][i : i + 1, :]) for j in range(i + 1)] for i in range(8)]
        inv, w, roots = [], [], []
        f = [[None] * 8 for _ in range(8)]
        for t in range(8):
            pivot = e[t][t]
            inv.append(1.0 / pivot)
            root = lax.rsqrt(pivot)
            roots.append(root * (1.5 - 0.5 * pivot * root * root))
            for i in range(t + 1, 8):
                f[i][t] = e[i][t] * inv[t]
            for i in range(t + 1, 8):
                for j in range(t + 1, i + 1):
                    e[i][j] = e[i][j] - f[i][t] * e[j][t]
        for i in range(8):
            r = []
            for j in range(i):
                acc = f[i][j]
                for k in range(j + 1, i):
                    acc = acc + f[i][k] * w[k][j]
                r.append(-acc)
            w.append(r)
        rows, vrows = s[b], v[b]
        new, vnew, scale = rows, vrows, roots[0]
        for i in range(1, 8):
            scale = jnp.where(sub == i, roots[i], scale)
        for j in range(7):
            c = jnp.zeros((8, 128), f32)
            for i in range(j + 1, 8):
                c = jnp.where(sub == i, w[i][j], c)
            new = new + c * full(rows[j : j + 1, :])
            vnew = vnew + c * full(vrows[j : j + 1, :])
        u_ref[8 * b : 8 * b + 8, :] = jnp.where(lane >= sub + 8 * b, new * scale, 0.0)
        w_ref[8 * b : 8 * b + 8, :] = vnew * scale
        if b == 15:
            break
        wi = [[w[t][j] * inv[t] for j in range(t)] for t in range(8)]
        brow = [full(new[t : t + 1, :]) for t in range(8)]
        bvrow = [full(vnew[t : t + 1, :]) for t in range(8)]
        for g in range(b + 1, 16):
            c = [full(s[g][:, 8 * b + j : 8 * b + j + 1]) for j in range(8)]
            for t in range(8):
                m = inv[t] * c[t]
                for j in range(t):
                    m = m + wi[t][j] * c[j]
                s[g] = s[g] - m * brow[t]
                v[g] = v[g] - m * bvrow[t]


def factor_kernel(index_ref, *refs):
    pieces, (l_ref, x_ref, a_ref, u_ref, w_ref) = refs[:8], refs[8:]
    for part, ref in enumerate(pieces):
        for n in range(4):
            j = index_ref[part * 4 + n]
            cols = pl.ds(pl.multiple_of(j % 4 * 256, 256), 256)
            for tile in range(8):
                rows = pl.ds(pl.multiple_of(tile * 128 + j // 4 * 16, 16), 16)
                a_ref[rows, cols] = ref[n, tile]
    l_ref[...] = jnp.zeros_like(l_ref)
    x_ref[...] = jnp.zeros_like(x_ref)
    for i in range(8):
        for j in range(i + 1):
            bi, bj = slice(128 * i, 128 * i + 128), slice(128 * j, 128 * j + 128)
            a_ref[bi, bj] = 0.5 * (a_ref[bi, bj] + a_ref[bj, bi].T)

    def step(b, carry):
        at = pl.ds(pl.multiple_of(b * 128, 128), 128)
        factor_block(a_ref[at, at], u_ref, w_ref)
        w = w_ref[...]
        l_ref[at, at] = u_ref[...].T
        x_ref[at, at] = w
        for n in range(8):

            @pl.when(b == n)
            def _():
                here = slice(128 * n, 128 * n + 128)
                if n < 7:
                    below = slice(128 * n + 128, PANEL)
                    low = times_transposed(a_ref[below, here], w)
                    l_ref[below, here] = low
                    for j in range(n + 1, 8, 2):
                        wide = min(256, PANEL - 128 * j)
                        rows, cols = slice(128 * j, PANEL), slice(128 * j, 128 * j + wide)
                        off = 128 * (j - n - 1)
                        a_ref[rows, cols] = a_ref[rows, cols] - times_transposed(
                            low[off:], low[off : off + wide]
                        )
                if n > 0:
                    done = slice(0, 128 * n)
                    x_ref[here, done] = -times(w, times(l_ref[here, done], x_ref[done, done]))

        return carry

    lax.fori_loop(0, 8, step, 0)


def factor(index, pieces):
    whole = pl.BlockSpec(memory_space=pltpu.VMEM)
    return pl.pallas_call(
        factor_kernel,
        in_specs=[pl.BlockSpec(memory_space=pltpu.SMEM)] + [whole] * 8,
        out_specs=[whole, whole],
        out_shape=[jax.ShapeDtypeStruct((PANEL, PANEL), f32)] * 2,
        scratch_shapes=[
            pltpu.VMEM((PANEL, PANEL), f32),
            pltpu.VMEM((128, 128), f32),
            pltpu.VMEM((128, 128), f32),
        ],
        compiler_params=pltpu.CompilerParams(vmem_limit_bytes=40 * MIB),
        cost_estimate=pl.CostEstimate(
            flops=7 * 10**10, bytes_accessed=12 * MIB, transcendentals=0
        ),
        name="factor_and_invert",
    )(index, *pieces)


def assemble_kernel(front_ref, got_ref, out_ref):
    for tile in range(2):
        for jc in range(4):
            cols = slice(jc * 256, jc * 256 + 256)
            sums = got_ref[:, jc, tile].reshape(128, 256)
            out_ref[tile, :, cols] = front_ref[tile, 0, :, cols] + sums


def assemble(front, got):
    k = front.shape[0]
    return pl.pallas_call(
        assemble_kernel,
        grid=(k // 2,),
        in_specs=[
            pl.BlockSpec((2, 1, 128, PANEL), lambda i: (i, 0, 0, 0)),
            pl.BlockSpec((8, 4, 2, 16, 256), lambda i: (0, 0, i, 0, 0)),
        ],
        out_specs=pl.BlockSpec((2, 128, PANEL), lambda i: (i, 0, 0)),
        out_shape=jax.ShapeDtypeStruct((k, 128, PANEL), f32),
        compiler_params=pltpu.CompilerParams(vmem_limit_bytes=56 * MIB),
        cost_estimate=pl.CostEstimate(
            flops=k * 128 * PANEL, bytes_accessed=12 * MIB, transcendentals=0
        ),
        name="assemble_panel",
    )(front, got)


def finish_kernel(order_ref, index_ref, panel_ref, lower_ref, top_ref, front_ref, got_ref, *refs):
    spread, pieces, (out_ref, slab_ref, rows_ref) = refs[:5], refs[5:13], refs[13:]
    step = pl.program_id(0)
    tiles = panel_ref.shape[0]
    leading = order_ref[4] == 0

    @pl.when(step == 0)
    def _():
        for part, ref in enumerate(pieces):
            for n in range(4):
                j = index_ref[part * 4 + n]
                for q in range(3):
                    at = (j % 4 * 3 + q) * 128 + j // 4 * 16
                    slab_ref[pl.ds(pl.multiple_of(at, 16), 16), :] = ref[n, q]

    for number in range(4):

        @pl.when(step == number)
        def _():
            if number == 2:
                rows_ref[:128, :] = spread[2][...]
                rows_ref[128:, :] = spread[3][...]
            else:
                rows_ref[...] = spread[number + number // 3][...]

    rows = rows_ref[...]

    @pl.when(leading)
    def _():
        out_ref[:, 0, :, :PANEL] = lower_ref[...]

    @pl.when(leading & (order_ref[step] == 0) & (order_ref[5] < 8))
    def _():
        out_ref[0, 0, :, :PANEL] = top_ref[...]

    @pl.when(jnp.logical_not(leading))
    def _():
        update = times_transposed(rows, slab_ref[:PANEL, :], None)
        out_ref[:, 0, :, :PANEL] = panel_ref[...] - update.reshape(tiles, 128, PANEL)

    update = times_transposed(rows, slab_ref[PANEL:, :], None).reshape(tiles, 128, -1)
    for jc in range(4):
        for tile in range(tiles):
            cols = slice(jc * 128, jc * 128 + 128)
            sums = got_ref[:, jc, tile].reshape(128, 128)
            out_ref[tile, 0, :, PANEL + jc * 128 : PANEL + jc * 128 + 128] = (
                front_ref[tile, 0, :, cols] + sums - update[tile, :, cols]
            )


def finish(order, index, panel, lower, top, front, got, spread, pieces):
    k, _, _, width = front.shape
    step = k // 4
    return pl.pallas_call(
        finish_kernel,
        grid_spec=pltpu.PrefetchScalarGridSpec(
            num_scalar_prefetch=2,
            grid=(4,),
            in_specs=[
                pl.BlockSpec((step, 128, PANEL), lambda i, o, _: (o[i], 0, 0)),
                pl.BlockSpec((step, 128, PANEL), lambda i, o, _: (o[i], 0, 0)),
                pl.BlockSpec((128, PANEL), lambda i, o, _: (0, 0)),
                pl.BlockSpec((step, 1, 128, 512), lambda i, o, _: (o[i], 0, 0, 2)),
                pl.BlockSpec((8, 4, step, 16, 128), lambda i, o, _: (0, 0, o[i], 0, 0)),
            ]
            + [pl.BlockSpec(x.shape, lambda i, o, _: (0, 0)) for x in spread]
            + [pl.BlockSpec(x.shape, lambda i, o, _: (0, 0, 0, 0)) for x in pieces],
            out_specs=pl.BlockSpec((step, 1, 128, width), lambda i, o, _: (o[i], 0, 0, 0)),
            scratch_shapes=[
                pltpu.VMEM((width, PANEL), bf16),
                pltpu.VMEM((step * 128, PANEL), bf16),
            ],
        ),
        out_shape=jax.ShapeDtypeStruct(front.shape, f32),
        compiler_params=pltpu.CompilerParams(vmem_limit_bytes=60 * MIB),
        cost_estimate=pl.CostEstimate(
            flops=2 * k * 128 * width * PANEL,
            bytes_accessed=28 * MIB,
            transcendentals=0,
        ),
        name="trailing_update",
    )(order, index, panel, lower, top, front, got, *spread, *pieces)


def exchange(x):
    return lax.all_to_all(x, "row", split_axis=0, concat_axis=0, tiled=True)


def row_number(x, z, core):
    return (x % 4 * 4 + z % 4) * 2 + core


def ring_stage(x, stage):
    parts = [x]
    for by in range(1, 4):
        moves = []
        for chip in range(16):
            for core in range(2):
                along_z = core == stage
                to = row_number(
                    chip // 4 + (0 if along_z else by), chip % 4 + (by if along_z else 0), core
                )
                moves.append((chip * 2 + core, to))
        parts.append(lax.ppermute(x, "row", moves))
    return parts


def with_cores(mine):
    return mine + [lax.ppermute(part, "row", [(r, r ^ 1) for r in range(32)]) for part in mine]


def gathered_index(row_index):
    number = jnp.arange(32, dtype=jnp.int32)
    half, outer, inner = number // 16, number // 4 % 4, number % 4
    core = (row_index + half) % 2
    chip = row_index // 2
    x = chip // 4 - jnp.where(core == 0, outer, inner) + 4
    z = chip % 4 - jnp.where(core == 0, inner, outer) + 4
    return row_number(x, z, core)


def exchange_by_permutes(x, row_index, other):
    rest = x.shape[1:]
    core, z, along = row_index % 2, row_index // 2 % 4, row_index // 8
    x = x.reshape((4, 4, 2) + rest)
    keep = jnp.where(core == 0, x[:, :, 0], x[:, :, 1])
    send = jnp.where(core == 0, x[:, :, 1], x[:, :, 0])
    x = jnp.stack([keep, lax.ppermute(send, "row", [(r, r ^ 1) for r in range(32)])])
    for stage, place_now in enumerate((z, along)):
        parts = []
        for by in range(4):
            part = lax.dynamic_index_in_dim(x, (place_now + by) % 4, x.ndim - len(rest) - 1, False)
            if by:
                moves = []
                for r in range(32):
                    there = (r // 8, r // 2 % 4 + by) if stage == 0 else (r // 8 + by, r // 2 % 4)
                    moves.append((r, row_number(*there, r % 2)))
                part = lax.ppermute(part, "row", moves)
            parts.append(part)
        x = jnp.stack(parts)
        if stage == 0:
            x, other = together(x, other)
    source = jnp.arange(32, dtype=jnp.int32)
    at = (along - source // 8 + 4) % 4 * 8 + (z - source // 2 % 4 + 4) % 4 * 2
    at = at + (core ^ (source % 2))
    return jnp.take(x.reshape((32,) + rest), at, axis=0, mode="clip"), other


def from_first(pieces, col_index):
    result = jnp.where(col_index == 0, pieces[0], 0)
    for c in range(1, len(pieces)):
        result = result + lax.ppermute(pieces[c], "col", [(0, c)])
    return result


def own_rows(tiles, row_index):
    tiles = tiles.reshape(4, 3, 16, 256)
    quarter = row_index % 4
    result = jnp.zeros((3, 16, PANEL), f32)
    for by in range(4):
        part = lax.dynamic_index_in_dim(tiles, quarter ^ by, 0, keepdims=False)
        if by:
            part = lax.ppermute(part, "row", [(r, r ^ by) for r in range(32)])
        result = lax.dynamic_update_slice(result, part, (0, 0, (quarter ^ by) * 256))
    return result.reshape(48, PANEL)


def together(*arrays):
    return lax.optimization_barrier(arrays)


def body(front, child_tiles, tile_parent, tile_rows, tile_count):
    row_index = lax.axis_index("row").astype(jnp.int32)
    col_index = lax.axis_index("col").astype(jnp.int32)
    slots = child_tiles.shape[0]
    index = gathered_index(row_index)
    live = jnp.arange(slots, dtype=jnp.int32) < tile_count[0]
    rows = jnp.where(live[:, None], tile_rows, -1)
    at = (tile_parent % 32) * 8 + tile_parent // 32

    early = front[:2, 0, :, :PANEL].reshape(2, 8, 16, 4, 256).transpose(1, 3, 0, 2, 4)
    at = jnp.pad(at.astype(f32).reshape(1, slots), ((0, 7), (0, 256 - slots)))
    early = jnp.concatenate(
        [early.reshape(32, 32, 256), jnp.broadcast_to(at[None], (32, 8, 256))], axis=1
    )
    sent_rest = place(rows, child_tiles, 128, 2).reshape(32, slots, 16, 128)
    early, sent_rest = exchange_by_permutes(early, row_index, sent_rest)
    at = early[:, 32, :slots].astype(jnp.int32).reshape(32 * slots)
    early = early[:, :32].reshape(32, 2, 16, 256)

    sent = place(rows, child_tiles, 256, 0).reshape(32, slots, 16, 256)
    got, sent_rest = together(exchange(sent), sent_rest)
    sums = collect(at, got).reshape(32, 8, 16, 256)

    tiles = (sums[:, :2] + early).transpose(1, 0, 2, 3).reshape(64, 16, 256)
    pieces = [jnp.concatenate([tiles[:8], tiles[12 * c : 12 * c + 12]]) for c in range(4)]
    piece = from_first(pieces, col_index)
    ring, part = together(jnp.stack(ring_stage(piece[:8], 0)), own_rows(piece[8:], row_index))
    diagonal = with_cores(ring_stage(ring, 1))

    got, sent_rest = together(exchange(sums), sent_rest)
    panel = assemble(front, got.reshape(8, 4, 8, 16, 256))
    own = from_first([panel[2 * c : 2 * c + 2] for c in range(4)], col_index)
    got_rest = exchange(sent_rest)

    factored, inverse = factor(index, diagonal)

    def rows_of_factor(start, count):
        start = jnp.minimum(start, PANEL - count)
        return lax.dynamic_slice_in_dim(factored, start, count, 0)

    top = rows_of_factor(row_index * 128, 128)
    known, tile = [top], 12 * col_index + 3 * (row_index % 4)
    for q in range(3):
        known.append(rows_of_factor((tile + q) * 128 + row_index // 4 * 16, 16))
    known = jnp.concatenate(known)
    inside = jnp.concatenate(
        [
            jnp.broadcast_to((row_index < 8) & (col_index == 0), (128,)),
            jnp.repeat(tile + jnp.arange(3, dtype=jnp.int32) < 8, 16, total_repeat_length=48),
        ]
    )
    solved = jnp.concatenate([own.reshape(256, PANEL), part])
    solved = times_transposed(solved, inverse)
    both = jnp.concatenate([solved[:128], solved[256:]])
    both = jnp.where(inside[:, None], known, both).astype(bf16)
    own = jnp.concatenate([both[:128], solved[128:256].astype(bf16)])
    part = both[128:].reshape(3, 16, PANEL)

    def turn(x, by):
        return lax.ppermute(x, "col", [(c, (c + by) % 4) for c in range(4)])

    before, behind = turn(own, 1), turn(own, 3)
    sums_rest = collect(at, got_rest, own, part)
    ring, sums_rest, before, behind = together(
        jnp.stack(ring_stage(part, 0)), sums_rest, before, behind
    )
    got_rest = exchange(sums_rest.reshape(32, 8, 16, 128)).reshape(8, 4, 8, 16, 128)
    lower = times_transposed(panel.reshape(8 * 128, PANEL), inverse).reshape(8, 128, PANEL)
    far = turn(before[:128], 1), turn(behind[128:], 3)
    *mine, lower, far_before, far_behind = together(*ring_stage(ring, 1), lower, *far)
    spread = [own, before, far_before, far_behind, behind]
    slab = with_cores(mine)

    order = (col_index + 4 - jnp.arange(4, dtype=jnp.int32)) % 4
    order = jnp.concatenate([order, jnp.stack([col_index, row_index])])
    return finish(order, index, panel, lower, top, front, got_rest, spread, slab)


def solution(mesh):
    placed = (
        P(None, "row", None, "col"),
        P("row", None, "col"),
        P("row"),
        P("row", None),
        P("row"),
    )
    return jax.shard_map(
        body, mesh=mesh, in_specs=placed, out_specs=P(None, "row", None, "col"), check_vma=False
    )
```
